128 devices in a mesh: seq: 32 (over y, z_lo, x), loop: 4 (over z_hi, core).
Axes of the slice: x: 4, y: 4, z: 4 (z_hi: 2, z_lo: 2; z = z_hi * 2 + z_lo), core: 2. Of those that a mesh axis runs over, the one named last changes fastest.
Arguments:
- events: bfloat16 [4, 16384, 512], P('loop', 'seq'), may hold values from -6 to 6
- carried: float32 [4, 16384, 512], P('loop', 'seq'), may hold values from -48 to 48
- positions: int32 [4, 16384], P('loop', 'seq'), may hold values from 0 to 8192, as said below
- neg_ids: int32 [4, 32, 4096], P('loop', 'seq'), may hold values from 0 to 524287, as said below
- pos_ids: int32 [4, 16384], P('loop', 'seq'), may hold values from 0 to 524287, as said below
- in_gain: float32 [512], replicated, may hold values from 0.5 to 1.5
- w_in: bfloat16 [512, 2048], replicated, may hold values from -0.25 to 0.25
- attn_gain: float32 [512], replicated, may hold values from 0.5 to 1.5
- w_out: bfloat16 [512, 512], replicated, may hold values from -0.25 to 0.25
- table: bfloat16 [524288, 512], P(('seq', 'loop')), may hold values from -0.25 to 0.25
Outputs:
- token_losses: float32 [4, 16384], P('loop', 'seq')
- grad_hidden: bfloat16 [4, 16384, 512], P('loop', 'seq')
- grad_table: float32 [524288, 512], P(('seq', 'loop'))
The draws below stay inside these ranges and needn't reach their ends.
Inputs may be any that keep to these rules, and one draw needn't show every extreme that they name: `positions`: nondecreasing along each history from 0 at its first event, rising by 0 or 1 from one event to the next. `neg_ids`: slot k of every block names a row held by table device k // 32, the table's rows lying in runs of 4096 over the devices in the order seq+loop. `pos_ids`: the 512 events of one block name rows of one table device at most 8 times; in every block some table device is named exactly 8 times.
All inputs are finite; a program needn't handle non-finite values.
Results may differ from the reference program's by a relative error of at most 0.005.
The reference program's roundings to bfloat16 on the way count: a program that leaves them out, or rounds other values in their place, can miss the bound.
Values may be sent and summed in bfloat16 or wider, within the bound.
A program may use at most 128 MiB of HBM per device.

```python
import jax
import jax.numpy as jnp
from jax import lax

HEADS = 8
DH = 64
D = 512
TOK_DEV = 512
NEG = 4096
ROWS_DEV = 4096
WINDOW = 4
BATCH = 4
SEQLEN = 16384
ITEMS = 524288
N_SEQ = 32
DEVICES = 128


def history_steps(key):
    order = jax.random.permutation(key, SEQLEN - 1)
    rising = (order < SEQLEN // 2).astype(jnp.int32)
    return jnp.concatenate([jnp.zeros((1,), jnp.int32), rising])


def draw_positions(key, part):
    key = jax.random.fold_in(key, 11)
    row_keys = jax.random.split(key, BATCH)
    rising = jax.vmap(history_steps)(row_keys)
    return jnp.cumsum(rising, axis=1).astype(jnp.int32)


def draw_neg_ids(key, part):
    key = jax.random.fold_in(key, 23)
    owner = (jnp.arange(NEG, dtype=jnp.int32) // (NEG // DEVICES))[None, None, :]
    local = jax.random.randint(key, (BATCH, N_SEQ, NEG), 0, ROWS_DEV)
    return (owner * ROWS_DEV + local).astype(jnp.int32)


def block_positives(key):
    first, second, third, fourth = jax.random.split(key, 4)
    half = 2 * TOK_DEV // DEVICES // 2
    spread = jax.random.randint(first, (DEVICES // 2,), 0, half + 1)
    spread = spread.at[0].set(half)
    counts = jnp.stack([half + spread, half - spread], axis=1).reshape(DEVICES)
    bounds = jnp.cumsum(counts)
    slot_owner = jnp.sum((jnp.arange(TOK_DEV)[:, None] >= bounds[None, :]).astype(jnp.int32), axis=1)
    relabel = jax.random.permutation(second, DEVICES)
    owner = relabel[slot_owner]
    order = jax.random.permutation(third, TOK_DEV)
    owner = owner[order]
    local = jax.random.randint(fourth, (TOK_DEV,), 0, ROWS_DEV)
    return (owner * ROWS_DEV + local).astype(jnp.int32)


def draw_pos_ids(key, part):
    key = jax.random.fold_in(key, 37)
    block_keys = jax.random.split(key, BATCH * N_SEQ)
    chosen = jax.vmap(block_positives)(block_keys)
    return chosen.reshape(BATCH, SEQLEN)


def shard_levels(key, dims, shards, least, high):
    factor_of, own = 1.0, jax.random.fold_in(key, 6)
    for position, shards_of in shards:
        heights = jnp.exp(jax.random.uniform(jax.random.fold_in(own, position), (shards_of,), jnp.float32, least / len(shards), high / len(shards)))
        factor_of = factor_of * jnp.repeat(heights, dims[position] // shards_of).reshape([-1 if axis == position else 1 for axis in range(len(dims))])
    return factor_of


def bell_draw(rng, extent, scale, most, shards=(), held_as=jnp.bfloat16):
    values = jax.random.normal(rng, extent, jnp.float32) * scale
    if len(shards) > 0:
        values = shard_levels(rng, extent, shards, -0.22, 0.18) * values
    return jnp.clip(values, min=-most, max=most).astype(held_as)


def setup_inputs(seed: int = 0) -> dict:
    key_list = jax.random.split(jax.random.key(seed), 11)
    events = bell_draw(key_list[0], (BATCH, SEQLEN, D), 1.0, 6.0, ((0, 4), (1, 32)))
    carried = bell_draw(key_list[1], (BATCH, SEQLEN, D), 8.0, 48.0, ((0, 4), (1, 32)), jnp.float32)
    positions = draw_positions(jax.random.fold_in(key_list[10], 71), 0)
    neg_ids = draw_neg_ids(jax.random.fold_in(key_list[10], 71), 0)
    pos_ids = draw_pos_ids(jax.random.fold_in(key_list[10], 71), 0)
    in_gain = jnp.clip(1.0 + 0.1 * jax.random.normal(key_list[5], (D,), jnp.float32), 0.5, 1.5)
    w_in = bell_draw(key_list[6], (D, 4 * D), D ** -0.5, 0.25)
    attn_gain = jnp.clip(1.0 + 0.1 * jax.random.normal(key_list[7], (D,), jnp.float32), 0.5, 1.5)
    w_out = bell_draw(key_list[8], (D, D), D ** -0.5, 0.25)
    table = bell_draw(key_list[9], (ITEMS, D), D ** -0.5, 0.25, ((0, 128),))
    return dict(events=events, carried=carried, positions=positions, neg_ids=neg_ids, pos_ids=pos_ids, in_gain=in_gain, w_in=w_in, attn_gain=attn_gain, w_out=w_out, table=table)


SOFTMAX_COOLING = 0.02
EPSILON = 1e-06

def rms_scale(values, gain):
    return values * lax.rsqrt(lax.optimization_barrier(jnp.mean(values * values, axis=-1, keepdims=True)) + EPSILON) * gain

def unit_rows(values):
    factor = lax.rsqrt(lax.optimization_barrier(jnp.sum(values * values, axis=-1, keepdims=True)) + EPSILON)
    return (values * factor, factor)

def unit_back(values, factor, upstream):
    direction = values * factor
    return factor * (upstream - direction * lax.optimization_barrier(jnp.sum(direction * upstream, axis=-1, keepdims=True)))

def sampled_loss(hidden, neg_rows, pos_rows, negatives, positives):
    hidden_wide = hidden.astype(jnp.float32)
    hidden_unit, hidden_factor = unit_rows(hidden_wide)
    state_reduced_precision = hidden_unit.astype(jnp.bfloat16)
    neg_wide = neg_rows.astype(jnp.float32)
    neg_unit, neg_factor = unit_rows(neg_wide)
    decoy_reduced_precision = neg_unit.astype(jnp.bfloat16)
    pos_wide = pos_rows.astype(jnp.float32)
    target_item_direction, pos_factor = unit_rows(pos_wide)
    decoy_raw_similarity = lax.dot_general(state_reduced_precision, decoy_reduced_precision, (((1,), (1,)), ((), ())), preferred_element_type=jnp.float32) / SOFTMAX_COOLING
    state_sent_home = lax.optimization_barrier(state_reduced_precision).astype(jnp.float32)
    target_raw_similarity = lax.optimization_barrier(jnp.sum(state_sent_home * target_item_direction, axis=-1)) / SOFTMAX_COOLING
    keeping = (negatives[None, :] != positives[:, None]).astype(jnp.float32)
    neg_exp = jnp.exp(decoy_raw_similarity) * keeping
    pos_exp = jnp.exp(target_raw_similarity)
    total = pos_exp + lax.optimization_barrier(jnp.sum(neg_exp, axis=1))
    token_loss = jnp.log(total) - target_raw_similarity
    decoy_softmax_chance = (neg_exp / total[:, None]).astype(jnp.bfloat16)
    target_softmax_chance = pos_exp / total - 1.0
    derivative_state_direction = (jnp.dot(decoy_softmax_chance, decoy_reduced_precision, preferred_element_type=jnp.float32) + target_softmax_chance[:, None] * target_item_direction) / SOFTMAX_COOLING
    derivative_decoy_direction = lax.dot_general(decoy_softmax_chance, state_reduced_precision, (((0,), (0,)), ((), ())), preferred_element_type=jnp.float32) / SOFTMAX_COOLING
    derivative_target_direction = target_softmax_chance[:, None] * state_sent_home / SOFTMAX_COOLING
    d_hidden = unit_back(hidden_wide, hidden_factor, derivative_state_direction).astype(jnp.bfloat16)
    d_neg = unit_back(neg_wide, neg_factor, derivative_decoy_direction).astype(jnp.bfloat16)
    d_pos = unit_back(pos_wide, pos_factor, derivative_target_direction).astype(jnp.bfloat16)
    return (token_loss, d_hidden, d_neg, d_pos)

def attend(queries, key_rows, value_rows, query_stamps, key_stamps):
    scores = jnp.einsum('thd,khd->htk', queries.astype(jnp.float32), key_rows.astype(jnp.float32)) * DH ** (-0.5)
    allowed = key_stamps[None, None, :] <= query_stamps[None, :, None]
    weights = jnp.where(allowed, jax.nn.silu(scores), 0.0).astype(jnp.bfloat16)
    weights = lax.optimization_barrier(weights)
    mixed = jnp.einsum('htk,khd->thd', weights.astype(jnp.float32), value_rows.astype(jnp.float32))
    return mixed.reshape(queries.shape[0], -1)

def reference(events, carried, positions, neg_ids, pos_ids, in_gain, w_in, attn_gain, w_out, table):
    width = HEADS * DH
    flat = events.reshape(-1, width)
    normed = rms_scale(flat.astype(jnp.float32), in_gain).astype(jnp.bfloat16)
    projected = jax.nn.silu(jnp.dot(normed, w_in, preferred_element_type=jnp.float32)).astype(jnp.bfloat16)
    projected = lax.optimization_barrier(projected).reshape(BATCH, N_SEQ, TOK_DEV, 4, HEADS, DH)
    padded = jnp.pad(projected, ((0, 0), (WINDOW - 1, 0), (0, 0), (0, 0), (0, 0), (0, 0)))
    stamps = positions.reshape(BATCH, N_SEQ, TOK_DEV)
    stamp_pad = jnp.pad(stamps, ((0, 0), (WINDOW - 1, 0), (0, 0)))
    event_blocks = events.reshape(BATCH, N_SEQ, TOK_DEV, width)
    carried_blocks = carried.reshape(BATCH, N_SEQ, TOK_DEV, width)
    pos_blocks = pos_ids.reshape(BATCH, N_SEQ, TOK_DEV)

    def one_block(grad_table, index):
        batch = (index // N_SEQ).astype(jnp.int32)
        shard = (index % N_SEQ).astype(jnp.int32)
        zero = jnp.zeros((), jnp.int32)
        own = projected[batch, shard]
        window_rows = lax.dynamic_slice(padded, (batch, shard, zero, zero, zero, zero), (1, WINDOW, TOK_DEV, 4, HEADS, DH))
        window_rows = window_rows.reshape(WINDOW * TOK_DEV, 4, HEADS, DH)
        window_stamps = lax.dynamic_slice(stamp_pad, (batch, shard, zero), (1, WINDOW, TOK_DEV)).reshape(-1)
        mixed = attend(own[:, 2], window_rows[:, 3], window_rows[:, 1], stamps[batch, shard], window_stamps)
        attended = carried_blocks[batch, shard] + mixed
        gated = (rms_scale(attended, attn_gain) * own[:, 0].reshape(TOK_DEV, width).astype(jnp.float32)).astype(jnp.bfloat16)
        hidden = (event_blocks[batch, shard].astype(jnp.float32) + jnp.dot(gated, w_out, preferred_element_type=jnp.float32)).astype(jnp.bfloat16)
        negatives = neg_ids[batch, shard]
        positives = pos_blocks[batch, shard]
        token_loss, d_hidden, d_neg, d_pos = sampled_loss(hidden, table[negatives], table[positives], negatives, positives)
        d_neg = lax.optimization_barrier(d_neg).astype(jnp.float32)
        d_pos = lax.optimization_barrier(d_pos).astype(jnp.float32)
        grad_table = grad_table.at[negatives].add(d_neg).at[positives].add(d_pos)
        return (grad_table, (token_loss, d_hidden))
    grad_table, outputs = lax.scan(one_block, jnp.zeros(table.shape, jnp.float32), jnp.arange(BATCH * N_SEQ, dtype=jnp.int32))
    losses, grads = outputs
    return (losses.reshape(BATCH, SEQLEN), grads.reshape(BATCH, SEQLEN, width), grad_table)
```

```python
import jax
import jax.numpy as jnp
from jax import lax
from jax.experimental import pallas as pl
from jax.experimental.pallas import tpu as pltpu
from jax.sharding import PartitionSpec as P

HEADS = 8
DH = 64
WINDOW = 4
WIDTH = HEADS * DH
LANES = 128
BANDS = WIDTH // LANES
TOKENS = 512
NEG = 4096
ROWS = 4096
DEVICES = 128
PER_OWNER = NEG // DEVICES
CAPACITY = 2 * TOKENS // DEVICES
ASKED = PER_OWNER + CAPACITY
MESSAGE = ASKED * BANDS
GROUP = 16
GROUPS = DEVICES // GROUP
GROUP_NEG = GROUP * PER_OWNER
GROUP_POS = GROUP * CAPACITY
NEG_LINES = PER_OWNER * BANDS

SHARPNESS = 50.0
LOG2E = 1.4426950408889634
EPSILON = 1e-06
F32 = jnp.float32
BF16 = jnp.bfloat16
NT = (((1,), (1,)), ((), ()))
TN = (((0,), (0,)), ((), ()))
BANK = 62 * 2**20


def silu(value):
    half = value * 0.5
    return half + half * jnp.tanh(half)


def row_sum(value):
    return jnp.sum(value, axis=-1, keepdims=True)


def normalise(rows, gain):
    wide = rows.astype(F32)
    scale = lax.rsqrt(row_sum(wide * wide) * (1.0 / WIDTH) + EPSILON)
    return (wide * scale * gain).astype(BF16)


def store_bands(ref, lead, value):
    for band in range(BANDS):
        ref[lead + (band,)] = value[:, band * LANES : (band + 1) * LANES]


def project_own(events, gain, w_in, gate, queries, keys, values):
    normed = normalise(events[...], gain[...])

    def column(index):
        part = jnp.dot(
            normed, w_in[:, index * WIDTH : (index + 1) * WIDTH], preferred_element_type=F32
        )
        return silu(part).astype(BF16)

    gate[...] = column(0)
    store_bands(values, (0,), column(1))
    store_bands(queries, (), (column(2).astype(F32) * 0.0625).astype(BF16))
    store_bands(keys, (0,), column(3))


def project_far(reach, rows, live, gain, w_in, keys, values):
    normed = normalise(rows, gain[...])

    def column(index):
        part = jnp.dot(
            normed, w_in[:, index * WIDTH : (index + 1) * WIDTH], preferred_element_type=F32
        )
        return (silu(part) * live).astype(BF16)

    store_bands(values, (reach,), column(1))
    store_bands(keys, (reach,), column(3))


def attend(stamp_cols, stamp_row, queries, keys, values, mixed):
    allowed = stamp_row[...] <= stamp_cols[:, :1]
    first = lax.broadcasted_iota(jnp.int32, (TOKENS, LANES), 1) < DH

    def pair(band, _):
        both = queries[band].astype(F32)
        parts = [
            jnp.where(first, both, 0.0).astype(BF16),
            jnp.where(first, 0.0, both).astype(BF16),
        ]

        def block(index, own):
            outs = []
            for part in parts:
                half = lax.dot_general(part, keys[index, band], NT, preferred_element_type=F32)
                weight = half + half * jnp.tanh(half)
                if own:
                    weight = jnp.where(allowed, weight, 0.0)
                outs.append(
                    jnp.dot(weight.astype(BF16), values[index, band], preferred_element_type=F32)
                )
            return jnp.where(first, outs[0], outs[1])

        mixed[band] = block(0, True)

        def later(index, _):
            mixed[band] += block(index, False)
            return 0

        lax.fori_loop(1, WINDOW, later, 0)
        return 0

    lax.fori_loop(0, BANDS, pair, 0)


def finish_hidden(events, carried, gain, w_out, gate, mixed, hidden):
    parts = [
        carried[:, band * LANES : (band + 1) * LANES] + mixed[band] for band in range(BANDS)
    ]
    squares = sum(row_sum(part * part) for part in parts)
    scale = lax.rsqrt(squares * (1.0 / WIDTH) + EPSILON)
    attended = jnp.concatenate(parts, axis=1)
    gated = (attended * scale * gain[...] * gate[...].astype(F32)).astype(BF16)
    hidden[...] = (
        events[...].astype(F32) + jnp.dot(gated, w_out[...], preferred_element_type=F32)
    ).astype(BF16)


def widen_table(table, lines):
    step = 256

    def part(index, _):
        start = pl.multiple_of(index * step, step)
        rows = table[pl.ds(start, step), :].astype(F32)
        for band in range(BANDS):
            lines[pl.ds(start * BANDS + band, step, stride=BANDS), :] = rows[
                :, band * LANES : (band + 1) * LANES
            ]
        return 0

    lax.fori_loop(0, ROWS // step, part, 0)


def answer(asked, lines, stage, message, peer):
    for slot in range(ASKED):
        row = jnp.maximum(asked[peer, slot], 0)
        stage[pl.ds(slot * BANDS, BANDS), :] = lines[pl.ds(row * BANDS, BANDS), :]
    for band in range(BANDS):
        message[peer, pl.ds(band * PER_OWNER, PER_OWNER), :] = stage[
            pl.ds(band, PER_OWNER, stride=BANDS), :
        ].astype(BF16)
    tail = [
        stage[pl.ds(NEG_LINES + band, CAPACITY, stride=BANDS), :] for band in range(BANDS)
    ]
    message[peer, pl.ds(NEG_LINES, CAPACITY * BANDS), :] = jnp.concatenate(tail, axis=0).astype(
        BF16
    )


def neg_rows(message, group):
    start = pl.multiple_of(group * GROUP, GROUP)
    parts = [
        message[pl.ds(start, GROUP), pl.ds(band * PER_OWNER, PER_OWNER), :].reshape(
            GROUP_NEG, LANES
        )
        for band in range(BANDS)
    ]
    return jnp.concatenate(parts, axis=1)


def pos_rows(message, group):
    start = pl.multiple_of(group * GROUP, GROUP)
    block = message[pl.ds(start, GROUP), pl.ds(NEG_LINES, CAPACITY * BANDS), :].astype(F32)
    block = block.reshape(GROUP, BANDS, CAPACITY, LANES)
    parts = [block[:, band].reshape(GROUP_POS, LANES) for band in range(BANDS)]
    return jnp.concatenate(parts, axis=1)


def unit_hidden(hidden, hidden_unit):
    wide = hidden[...].astype(F32)
    scale = lax.rsqrt(row_sum(wide * wide) + EPSILON)
    hidden_unit[...] = (wide * scale).astype(BF16)


def pick(slot_cols, group):
    lane = lax.broadcasted_iota(jnp.int32, (TOKENS, GROUP_POS), 1) + group * GROUP_POS
    return jnp.where(slot_cols[...] == lane, 1.0, 0.0).astype(BF16)


def share_rows(group, band):
    return pl.ds(pl.multiple_of((group * BANDS + band) * TOKENS, TOKENS), TOKENS)


def unit_rows(group):
    return pl.ds(pl.multiple_of(group * GROUP_NEG, GROUP_NEG), GROUP_NEG)


def meet_group(group, message, neg_ids, pos_cols, slot_cols, hidden_unit, units, shares, sums, targets):
    wide = neg_rows(message, group).astype(F32)
    scale = lax.rsqrt(row_sum(wide * wide) + EPSILON)
    unit = (wide * scale).astype(BF16)
    units[unit_rows(group), :] = unit
    logits = lax.dot_general(hidden_unit[...], unit, NT, preferred_element_type=F32)
    total = sums[...]
    for band in range(BANDS):
        keep = neg_ids[pl.ds(group * BANDS + band, 1), :] != pos_cols[...]
        near = logits[:, band * LANES : (band + 1) * LANES]
        grown = jnp.where(keep, jnp.exp2(near * (SHARPNESS * LOG2E)), 0.0)
        shares[share_rows(group, band), :] = grown
        total = total + grown
    sums[...] = total
    targets[...] += jnp.dot(
        pick(slot_cols, group),
        pos_rows(message, group).astype(BF16),
        preferred_element_type=F32,
    )


def settle(hidden_unit, sums, targets, loss, inverse):
    state = hidden_unit[...].astype(F32)
    wide = targets[...]
    scale = lax.rsqrt(row_sum(wide * wide) + EPSILON)
    unit = wide * scale
    logit = row_sum(state * unit) * SHARPNESS
    grown = jnp.exp(logit)
    total = grown + row_sum(sums[...])
    lost = jnp.broadcast_to(jnp.log(total) - logit, (TOKENS, LANES))
    for part in range(TOKENS // LANES):
        loss[pl.ds(part, 1), :] = lost[part * LANES : (part + 1) * LANES].T[:1]
    share = grown / total - 1.0
    inverse[...] = jnp.broadcast_to(1.0 / total, (TOKENS, LANES))
    upstream = (share * SHARPNESS) * state
    back = scale * (upstream - unit * row_sum(unit * upstream))
    targets[...] = (share * SHARPNESS) * unit
    return back.astype(BF16)


def return_group(group, message, slot_cols, hidden_unit, units, shares, inverse, d_pos, d_state, out):
    share = jnp.concatenate(
        [
            (shares[share_rows(group, band), :] * inverse[...]).astype(BF16)
            for band in range(BANDS)
        ],
        axis=1,
    )
    wide = neg_rows(message, group).astype(F32)
    scale = lax.rsqrt(row_sum(wide * wide) + EPSILON)
    unit = wide * scale
    upstream = (
        lax.dot_general(share, hidden_unit[...], TN, preferred_element_type=F32) * SHARPNESS
    )
    back = (scale * (upstream - unit * row_sum(unit * upstream))).astype(BF16)
    start = pl.multiple_of(group * GROUP, GROUP)
    for band in range(BANDS):
        out[pl.ds(start, GROUP), pl.ds(band * PER_OWNER, PER_OWNER), :] = back[
            :, band * LANES : (band + 1) * LANES
        ].reshape(GROUP, PER_OWNER, LANES)
    returned = lax.dot_general(pick(slot_cols, group), d_pos[...], TN, preferred_element_type=F32)
    parts = [
        returned[:, band * LANES : (band + 1) * LANES].reshape(GROUP, 1, CAPACITY, LANES)
        for band in range(BANDS)
    ]
    out[pl.ds(start, GROUP), pl.ds(NEG_LINES, CAPACITY * BANDS), :] = (
        jnp.concatenate(parts, axis=1).reshape(GROUP, CAPACITY * BANDS, LANES).astype(BF16)
    )
    d_state[...] += jnp.dot(share, units[unit_rows(group), :], preferred_element_type=F32)


def hidden_back(hidden, d_state, targets, grad):
    wide = hidden[...].astype(F32)
    scale = lax.rsqrt(row_sum(wide * wide) + EPSILON)
    unit = wide * scale
    upstream = d_state[...] * SHARPNESS + targets[...]
    grad[...] = (scale * (upstream - unit * row_sum(unit * upstream))).astype(BF16)


def add_group(group, message, neg_asked, pos_asked, total, done):
    negs = neg_rows(message, group)
    poss = pos_rows(message, group).astype(BF16)
    step = 512

    def tile(index, _):
        start = pl.multiple_of(index * step, step)
        row = lax.broadcasted_iota(jnp.int32, (step, LANES), 0) + start

        def hits(asked, line):
            return jnp.where(row == asked[pl.ds(line, 1), :], 1.0, 0.0).astype(BF16)

        wide = jnp.concatenate(
            [hits(neg_asked, group * BANDS + band) for band in range(BANDS)], axis=1
        )
        part = jnp.dot(wide, negs, preferred_element_type=F32)
        part += jnp.dot(hits(pos_asked, group), poss, preferred_element_type=F32)
        total[pl.ds(start, step), :] += part
        done(start, step)
        return 0

    lax.fori_loop(0, ROWS // step, tile, 0)


SEQ_BITS = ("x0", "x1", "zl", "y0", "y1")
LOOP_BITS = ("c", "zh")
ITEM_FLIPS = (("y0", "zh", "c"), ("x0", "y1"), ("zl", "c"), ("x1", "zh"))
GROUP_FLIPS = ("c", "zh", "y1")


def own_bits():
    seq, loop = lax.axis_index("seq"), lax.axis_index("loop")
    bits = {name: lax.rem(lax.div(seq, 2**at), 2) for at, name in enumerate(SEQ_BITS)}
    bits.update({name: lax.rem(lax.div(loop, 2**at), 2) for at, name in enumerate(LOOP_BITS)})
    return bits


def partners(group):
    bits = own_bits()
    for at, name in enumerate(GROUP_FLIPS):
        turn = lax.rem(lax.div(group, 2**at), 2)
        bits[name] = bits[name] + turn - 2 * bits[name] * turn
    seq = sum(bits[name] * 2**at for at, name in enumerate(SEQ_BITS))
    loop = sum(bits[name] * 2**at for at, name in enumerate(LOOP_BITS))
    seq_turn = {name: (1 - 2 * bits[name]) * 2**at for at, name in enumerate(SEQ_BITS)}
    loop_turn = {name: (1 - 2 * bits[name]) * 2**at for at, name in enumerate(LOOP_BITS)}
    met = []
    for item in range(GROUP):
        flips = set()
        for at, names in enumerate(ITEM_FLIPS):
            if item >> at & 1:
                flips ^= set(names)
        met.append(
            (
                sum((seq_turn[name] for name in SEQ_BITS if name in flips), seq),
                sum((loop_turn[name] for name in LOOP_BITS if name in flips), loop),
            )
        )
    return met


def each_partner(act):
    def one(group, _):
        for item, device in enumerate(partners(group)):
            slot = group * GROUP + item
            if item == 0:

                @pl.when(group > 0)
                def _():
                    act(slot, device)

            else:
                act(slot, device)
        return 0

    lax.fori_loop(0, GROUPS, one, 0)


def slot_of(owner):
    me = lax.axis_index("seq") * 4 + lax.axis_index("loop")
    apart = jnp.bitwise_xor(owner, me)
    names = LOOP_BITS + SEQ_BITS
    bit = {name: jnp.bitwise_and(jnp.right_shift(apart, at), 1) for at, name in enumerate(names)}
    first = jnp.bitwise_xor(jnp.bitwise_xor(bit["c"], bit["y0"]), bit["zl"])
    second = jnp.bitwise_xor(jnp.bitwise_xor(bit["zh"], bit["y0"]), bit["x1"])
    third = jnp.bitwise_xor(bit["y1"], bit["x0"])
    item = bit["y0"] + 2 * bit["x0"] + 4 * bit["zl"] + 8 * bit["x1"]
    return item + 16 * first + 32 * second + 64 * third


def columns_of(row, out):
    for part in range(TOKENS // LANES):
        square = jnp.broadcast_to(row[:, part * LANES : (part + 1) * LANES], (LANES, LANES))
        out[pl.ds(part * LANES, LANES), :] = square.T


def lanes_of(rows, out, count, skip):
    lane = lax.broadcasted_iota(jnp.int32, (GROUPS, LANES), 1)
    bands = count * GROUP // LANES
    share = LANES // count
    for band in range(bands):
        packed = jnp.zeros((GROUPS, LANES), jnp.int32)
        for part in range(share):
            some = rows[pl.ds(band * share + part, GROUPS, stride=GROUP), :]
            some = pltpu.roll(some, (part * count - skip) % LANES, axis=1)
            inside = (lane >= part * count) & (lane < (part + 1) * count)
            packed = jnp.where(inside, some, packed)
        out[pl.ds(band, GROUPS, stride=bands), :] = packed


def count_rows(flags):
    rows = flags.shape[0]
    while rows > 8:
        rows //= 2
        flags = flags[:rows] + flags[rows:]
    total = flags[:1]
    for row in range(1, 8):
        total = total + flags[row : row + 1]
    return total


def write_requests(negatives, pos_row, pos_cols, owned, met_ids, asks, slot_cols, rank_cols):
    lane = lax.broadcasted_iota(jnp.int32, (TOKENS, LANES), 1)
    line = lax.broadcasted_iota(jnp.int32, (TOKENS, LANES), 0)
    ids = pos_cols[...]
    slot = slot_of(jnp.right_shift(ids, 12))
    slot_row = slot_of(jnp.right_shift(pos_row[...], 12))
    ranks = []
    for part in range(TOKENS // LANES):
        near = slot_row[:, part * LANES : (part + 1) * LANES]
        earlier = (slot == near) & (line < lane + part * LANES)
        ranks.append(count_rows(jnp.where(earlier, 1, 0)))
    columns_of(jnp.concatenate(ranks, axis=1), rank_cols)
    rank = rank_cols[...]
    slot_cols[...] = slot * CAPACITY + rank
    named = jnp.where(slot == lane, jnp.bitwise_and(ids, ROWS - 1) + 1, 0)
    wanted = [jnp.zeros((PER_OWNER, LANES), jnp.int32)]
    for place in range(CAPACITY):
        wanted.append(count_rows(jnp.where(rank == place, named, 0)))
    wanted.append(jnp.zeros((LANES - ASKED, LANES), jnp.int32))
    wanted = jnp.concatenate(wanted, axis=0).T - 1
    share = LANES // PER_OWNER
    for part in range(share):
        owned[pl.ds(part, DEVICES // share, stride=share), :] = pltpu.roll(
            negatives[...], (LANES - part * PER_OWNER) % LANES, axis=1
        )

    def order(group, _):
        for item, (seq, loop) in enumerate(partners(group)):
            met_ids[pl.ds(group * GROUP + item, 1), :] = owned[pl.ds(seq * 4 + loop, 1), :]
        return 0

    lax.fori_loop(0, GROUPS, order, 0)
    slots = lax.broadcasted_iota(jnp.int32, (DEVICES, LANES), 1)
    asks[...] = jnp.where(
        slots < PER_OWNER, jnp.bitwise_and(met_ids[...], ROWS - 1), wanted
    )


def step_kernel(
    events_in,
    carried_in,
    stamp_row,
    negatives,
    pos_row,
    in_gain,
    w_in_in,
    attn_gain,
    w_out_in,
    table,
    loss_out,
    grad_out,
    total_out,
    events,
    carried,
    w_in,
    w_out,
    far,
    stamp_cols,
    pos_cols,
    slot_cols,
    rank_cols,
    owned,
    met_ids,
    asks,
    asked,
    asked_scalar,
    neg_ids,
    neg_asked,
    pos_asked,
    lines,
    units,
    stage,
    sent,
    answered,
    returned,
    gate,
    queries,
    keys,
    values,
    mixed,
    hidden,
    hidden_unit,
    sums,
    targets,
    inverse,
    d_pos,
    d_state,
    loss,
    grad,
    total,
    load_sems,
    local_sem,
    ask_send,
    ask_recv,
    halo_send,
    halo_recv,
    row_send,
    row_recv,
    back_send,
    back_recv,
    out_sems,
):
    seq, loop = lax.axis_index("seq"), lax.axis_index("loop")
    barrier = pltpu.get_barrier_semaphore()
    each_partner(
        lambda slot, device: pl.semaphore_signal(
            barrier, inc=1, device_id=device, device_id_type=pl.DeviceIdType.MESH
        )
    )
    loads = [
        pltpu.make_async_copy(source, target, load_sems.at[at])
        for at, (source, target) in enumerate(
            [
                (events_in, events),
                (table, units),
                (w_in_in, w_in),
                (w_out_in, w_out),
                (carried_in, carried),
            ]
        )
    ]
    for load in loads:
        load.start()

    def to_partner(source, target, send, recv, device):
        return pltpu.make_async_remote_copy(
            src_ref=source,
            dst_ref=target,
            send_sem=send,
            recv_sem=recv,
            device_id=device,
            device_id_type=pl.DeviceIdType.MESH,
        )

    other = (seq, loop + 1 - 2 * lax.rem(loop, 2))

    def expect(buffer, send, recv):
        return to_partner(buffer, buffer, send, recv, other)

    columns_of(pos_row, pos_cols)
    columns_of(stamp_row, stamp_cols)
    write_requests(
        negatives, pos_row, pos_cols, owned, met_ids, asks, slot_cols, rank_cols
    )
    asked[pl.ds(0, 1), :] = asks[pl.ds(0, 1), :]
    loads[0].wait()
    pl.semaphore_wait(barrier, DEVICES - 1)

    each_partner(
        lambda slot, device: to_partner(
            asks.at[pl.ds(slot, 1)], asked.at[pl.ds(slot, 1)], ask_send, ask_recv, device
        ).start()
    )
    halos = [
        to_partner(
            events,
            far.at[reach - 1],
            halo_send.at[reach - 1],
            halo_recv.at[reach - 1],
            (lax.rem(seq + reach, 32), loop),
        )
        for reach in range(1, WINDOW)
    ]
    for halo in halos:
        halo.start()

    lanes_of(met_ids, neg_ids, PER_OWNER, 0)
    loads[1].wait()
    widen_table(units, lines)
    loads[2].wait()
    project_own(events, in_gain, w_in, gate, queries, keys, values)
    sums[...] = jnp.zeros_like(sums)
    targets[...] = jnp.zeros_like(targets)
    d_state[...] = jnp.zeros_like(d_state)

    others = expect(asked.at[pl.ds(1, DEVICES - 1)], ask_send, ask_recv)
    others.wait_recv()
    scalars = pltpu.make_async_copy(asked, asked_scalar, local_sem)
    scalars.start()
    lanes_of(asked, neg_asked, PER_OWNER, 0)
    lanes_of(asked, pos_asked, CAPACITY, PER_OWNER)
    scalars.wait()

    def send_group(group, target, send, recv):
        for item, device in enumerate(partners(group)):
            slot = group * GROUP + item

            def start(slot=slot, device=device):
                to_partner(sent.at[slot], target.at[slot], send, recv.at[group], device).start()

            if item == 0:
                pl.when(group > 0)(start)
            else:
                start()

        @pl.when(group == 0)
        def _():
            mine = pltpu.make_async_copy(sent.at[0], target.at[0], local_sem)
            mine.start()
            mine.wait()

    def await_group(group, target, send, recv):
        @pl.when(group == 0)
        def _():
            expect(target.at[pl.ds(1, GROUP - 1)], send, recv.at[0]).wait_recv()

        @pl.when(group > 0)
        def _():
            expect(target.at[pl.ds(0, GROUP)], send, recv.at[group]).wait_recv()

    def answer_group(group, _):
        def one(item, _):
            answer(asked_scalar, lines, stage, sent, group * GROUP + item)
            return 0

        lax.fori_loop(0, GROUP, one, 0)
        send_group(group, answered, row_send, row_recv)
        return 0

    lax.fori_loop(0, GROUPS, answer_group, 0)

    def far_block(reach, _):
        expect(far.at[reach - 1], halo_send.at[reach - 1], halo_recv.at[reach - 1]).wait_recv()
        live = jnp.where(seq >= reach, 1.0, 0.0).astype(F32)
        project_far(reach, far[reach - 1], live, in_gain, w_in, keys, values)
        return 0

    lax.fori_loop(1, WINDOW, far_block, 0)
    attend(stamp_cols, stamp_row, queries, keys, values, mixed)
    loads[3].wait()
    loads[4].wait()
    finish_hidden(events, carried, attn_gain, w_out, gate, mixed, hidden)
    unit_hidden(hidden, hidden_unit)

    def meet(group, _):
        await_group(group, answered, row_send, row_recv)
        meet_group(
            group, answered, neg_ids, pos_cols, slot_cols, hidden_unit, units, lines, sums, targets
        )
        return 0

    lax.fori_loop(0, GROUPS, meet, 0)
    d_pos[...] = settle(hidden_unit, sums, targets, loss, inverse)
    expect(sent.at[pl.ds(0, DEVICES - 1)], row_send, row_recv.at[0]).wait_send()

    def back(group, _):
        return_group(
            group, answered, slot_cols, hidden_unit, units, lines, inverse, d_pos, d_state, sent
        )
        send_group(group, returned, back_send, back_recv)
        return 0

    lax.fori_loop(0, GROUPS, back, 0)
    hidden_back(hidden, d_state, targets, grad)
    outs = [
        pltpu.make_async_copy(loss, loss_out, out_sems.at[0]),
        pltpu.make_async_copy(grad, grad_out, out_sems.at[1]),
    ]
    for out in outs:
        out.start()
    total[...] = jnp.zeros_like(total)

    def collect(group, _):
        await_group(group, returned, back_send, back_recv)
        add_group(group, returned, neg_asked, pos_asked, total, lambda start, step: None)
        return 0

    lax.fori_loop(0, GROUPS, collect, 0)
    outs.append(pltpu.make_async_copy(total, total_out, out_sems.at[2]))
    outs[2].start()
    others.wait_send()
    for halo in halos:
        halo.wait_send()
    expect(sent.at[pl.ds(0, DEVICES - 1)], back_send, back_recv.at[0]).wait_send()
    for out in outs:
        out.wait()


def whole(kind, shape):
    return pltpu.VMEM(shape, kind)


def on_device(events, carried, positions, neg_ids, pos_ids, in_gain, w_in, attn_gain, w_out, table):
    inside = pl.BlockSpec(memory_space=pltpu.VMEM)
    outside = pl.BlockSpec(memory_space=pl.ANY)
    integers = jnp.int32
    loss, grad_hidden, grad_table = pl.pallas_call(
        step_kernel,
        out_shape=(
            jax.ShapeDtypeStruct((TOKENS // LANES, LANES), F32),
            jax.ShapeDtypeStruct((TOKENS, WIDTH), BF16),
            jax.ShapeDtypeStruct((ROWS, WIDTH), F32),
        ),
        in_specs=[
            outside,
            outside,
            inside,
            inside,
            inside,
            inside,
            outside,
            inside,
            outside,
            outside,
        ],
        out_specs=(outside, outside, outside),
        scratch_shapes=[
            whole(BF16, (TOKENS, WIDTH)),
            whole(F32, (TOKENS, WIDTH)),
            whole(BF16, (WIDTH, 4 * WIDTH)),
            whole(BF16, (WIDTH, WIDTH)),
            whole(BF16, (WINDOW - 1, TOKENS, WIDTH)),
            whole(integers, (TOKENS, LANES)),
            whole(integers, (TOKENS, LANES)),
            whole(integers, (TOKENS, LANES)),
            whole(integers, (TOKENS, LANES)),
            whole(integers, (DEVICES, LANES)),
            whole(integers, (DEVICES, LANES)),
            whole(integers, (DEVICES, LANES)),
            whole(integers, (DEVICES, LANES)),
            pltpu.SMEM((DEVICES, LANES), integers),
            whole(integers, (GROUPS * BANDS, LANES)),
            whole(integers, (GROUPS * BANDS, LANES)),
            whole(integers, (GROUPS, LANES)),
            whole(F32, (ROWS * BANDS, LANES)),
            whole(BF16, (ROWS, WIDTH)),
            whole(F32, (MESSAGE, LANES)),
            whole(BF16, (DEVICES, MESSAGE, LANES)),
            whole(BF16, (DEVICES, MESSAGE, LANES)),
            whole(BF16, (DEVICES, MESSAGE, LANES)),
            whole(BF16, (TOKENS, WIDTH)),
            whole(BF16, (BANDS, TOKENS, LANES)),
            whole(BF16, (WINDOW, BANDS, TOKENS, LANES)),
            whole(BF16, (WINDOW, BANDS, TOKENS, LANES)),
            whole(F32, (BANDS, TOKENS, LANES)),
            whole(BF16, (TOKENS, WIDTH)),
            whole(BF16, (TOKENS, WIDTH)),
            whole(F32, (TOKENS, LANES)),
            whole(F32, (TOKENS, WIDTH)),
            whole(F32, (TOKENS, LANES)),
            whole(BF16, (TOKENS, WIDTH)),
            whole(F32, (TOKENS, WIDTH)),
            whole(F32, (TOKENS // LANES, LANES)),
            whole(BF16, (TOKENS, WIDTH)),
            whole(F32, (ROWS, WIDTH)),
            pltpu.SemaphoreType.DMA((5,)),
            pltpu.SemaphoreType.DMA,
            pltpu.SemaphoreType.DMA,
            pltpu.SemaphoreType.DMA,
            pltpu.SemaphoreType.DMA((WINDOW - 1,)),
            pltpu.SemaphoreType.DMA((WINDOW - 1,)),
            pltpu.SemaphoreType.DMA,
            pltpu.SemaphoreType.DMA((GROUPS,)),
            pltpu.SemaphoreType.DMA,
            pltpu.SemaphoreType.DMA((GROUPS,)),
            pltpu.SemaphoreType.DMA((3,)),
        ],
        compiler_params=pltpu.CompilerParams(
            collective_id=0, has_side_effects=True, vmem_limit_bytes=BANK
        ),
        name="step",
    )(
        events[0],
        carried[0],
        positions,
        neg_ids.reshape(NEG // LANES, LANES),
        pos_ids,
        in_gain[None, :],
        w_in,
        attn_gain[None, :],
        w_out,
        table,
    )
    return (loss.reshape(1, TOKENS), grad_hidden[None], grad_table)


def solution(mesh):
    return jax.shard_map(
        on_device,
        mesh=mesh,
        in_specs=(
            P("loop", "seq", None),
            P("loop", "seq", None),
            P("loop", "seq"),
            P("loop", "seq", None),
            P("loop", "seq"),
            P(),
            P(),
            P(),
            P(),
            P(("seq", "loop"), None),
        ),
        out_specs=(P("loop", "seq"), P("loop", "seq", None), P(("seq", "loop"), None)),
        check_vma=False,
    )
```

```python
import functools

import jax
import jax.numpy as jnp
from jax import lax
from jax.experimental import pallas as pl
from jax.experimental.pallas import tpu as pltpu
from jax.sharding import PartitionSpec as P

HEADS = 8
DH = 64
WINDOW = 4
WIDTH = HEADS * DH
LANES = 128
BANDS = WIDTH // LANES
TOKENS = 512
NEG = 4096
ROWS = 4096
DEVICES = 128
PER_OWNER = NEG // DEVICES
CAPACITY = 2 * TOKENS // DEVICES
ASKED = PER_OWNER + CAPACITY
MESSAGE = ASKED * BANDS
GROUP = 16
GROUPS = DEVICES // GROUP
GROUP_NEG = GROUP * PER_OWNER
GROUP_POS = GROUP * CAPACITY
NEG_LINES = PER_OWNER * BANDS

SHARPNESS = 50.0
LOG2E = 1.4426950408889634
EPSILON = 1e-06
F32 = jnp.float32
BF16 = jnp.bfloat16
NT = (((1,), (1,)), ((), ()))
TN = (((0,), (0,)), ((), ()))
TILE = 1024
END_TILE = 512
CORNER_TURN, BACK_TURN, FORWARD_TURN = 1, 2, 3
BANK = 62 * 2**20


def silu(value):
    half = value * 0.5
    return half + half * jnp.tanh(half)


def row_sum(value):
    return jnp.sum(value, axis=-1, keepdims=True)


def normalise(rows, gain):
    wide = rows.astype(F32)
    scale = lax.rsqrt(row_sum(wide * wide) * (1.0 / WIDTH) + EPSILON)
    return (wide * scale * gain).astype(BF16)


def store_bands(ref, lead, value):
    for band in range(BANDS):
        ref[lead + (band,)] = value[:, band * LANES : (band + 1) * LANES]


def project_own(events, gain, w_in, gate, queries, keys, values):
    normed = normalise(events[...], gain[...])

    def column(index):
        part = jnp.dot(
            normed, w_in[:, index * WIDTH : (index + 1) * WIDTH], preferred_element_type=F32
        )
        return silu(part).astype(BF16)

    gate[...] = column(0)
    store_bands(values, (0,), column(1))
    store_bands(queries, (), (column(2).astype(F32) * 0.0625).astype(BF16))
    store_bands(keys, (0,), column(3))


def project_far(reach, rows, live, gain, w_in, keys, values):
    normed = normalise(rows, gain[...])

    def column(index):
        part = jnp.dot(
            normed, w_in[:, index * WIDTH : (index + 1) * WIDTH], preferred_element_type=F32
        )
        return (silu(part) * live).astype(BF16)

    store_bands(values, (reach,), column(1))
    store_bands(keys, (reach,), column(3))


def attend(stamp_cols, stamp_row, queries, keys, values, mixed):
    allowed = stamp_row[...] <= stamp_cols[:, :1]
    first = lax.broadcasted_iota(jnp.int32, (TOKENS, LANES), 1) < DH

    def pair(band, _):
        both = queries[band].astype(F32)
        parts = [
            jnp.where(first, both, 0.0).astype(BF16),
            jnp.where(first, 0.0, both).astype(BF16),
        ]

        def block(index, own):
            outs = []
            for part in parts:
                half = lax.dot_general(part, keys[index, band], NT, preferred_element_type=F32)
                weight = half + half * jnp.tanh(half)
                if own:
                    weight = jnp.where(allowed, weight, 0.0)
                outs.append(
                    jnp.dot(weight.astype(BF16), values[index, band], preferred_element_type=F32)
                )
            return jnp.where(first, outs[0], outs[1])

        mixed[band] = block(0, True)

        def later(index, _):
            mixed[band] += block(index, False)
            return 0

        lax.fori_loop(1, WINDOW, later, 0)
        return 0

    lax.fori_loop(0, BANDS, pair, 0)


def finish_hidden(events, carried, gain, w_out, gate, mixed, hidden):
    parts = [
        carried[:, band * LANES : (band + 1) * LANES] + mixed[band] for band in range(BANDS)
    ]
    squares = sum(row_sum(part * part) for part in parts)
    scale = lax.rsqrt(squares * (1.0 / WIDTH) + EPSILON)
    attended = jnp.concatenate(parts, axis=1)
    gated = (attended * scale * gain[...] * gate[...].astype(F32)).astype(BF16)
    hidden[...] = (
        events[...].astype(F32) + jnp.dot(gated, w_out[...], preferred_element_type=F32)
    ).astype(BF16)


def widen_table(table, lines):
    step = 256

    def part(index, _):
        start = pl.multiple_of(index * step, step)
        rows = table[pl.ds(start, step), :].astype(F32)
        for band in range(BANDS):
            lines[pl.ds(start * BANDS + band, step, stride=BANDS), :] = rows[
                :, band * LANES : (band + 1) * LANES
            ]
        return 0

    lax.fori_loop(0, ROWS // step, part, 0)


def answer(asked, lines, stage, message, peer):
    for slot in range(ASKED):
        row = jnp.maximum(asked[peer, slot], 0)
        stage[pl.ds(slot * BANDS, BANDS), :] = lines[pl.ds(row * BANDS, BANDS), :]
    for band in range(BANDS):
        message[peer, pl.ds(band * PER_OWNER, PER_OWNER), :] = stage[
            pl.ds(band, PER_OWNER, stride=BANDS), :
        ].astype(BF16)
    tail = [
        stage[pl.ds(NEG_LINES + band, CAPACITY, stride=BANDS), :] for band in range(BANDS)
    ]
    message[peer, pl.ds(NEG_LINES, CAPACITY * BANDS), :] = jnp.concatenate(tail, axis=0).astype(
        BF16
    )


def neg_rows(message, group):
    start = pl.multiple_of(group * GROUP, GROUP)
    parts = [
        message[pl.ds(start, GROUP), pl.ds(band * PER_OWNER, PER_OWNER), :].reshape(
            GROUP_NEG, LANES
        )
        for band in range(BANDS)
    ]
    return jnp.concatenate(parts, axis=1)


def pos_rows(message, group):
    start = pl.multiple_of(group * GROUP, GROUP)
    block = message[pl.ds(start, GROUP), pl.ds(NEG_LINES, CAPACITY * BANDS), :].astype(F32)
    block = block.reshape(GROUP, BANDS, CAPACITY, LANES)
    parts = [block[:, band].reshape(GROUP_POS, LANES) for band in range(BANDS)]
    return jnp.concatenate(parts, axis=1)


def unit_hidden(hidden, hidden_unit):
    wide = hidden[...].astype(F32)
    scale = lax.rsqrt(row_sum(wide * wide) + EPSILON)
    hidden_unit[...] = (wide * scale).astype(BF16)


def pick(slot_cols, group):
    lane = lax.broadcasted_iota(jnp.int32, (TOKENS, GROUP_POS), 1) + group * GROUP_POS
    return jnp.where(slot_cols[...] == lane, 1.0, 0.0).astype(BF16)


def share_rows(group, band):
    return pl.ds(pl.multiple_of((group * BANDS + band) * TOKENS, TOKENS), TOKENS)


def unit_rows(group):
    return pl.ds(pl.multiple_of(group * GROUP_NEG, GROUP_NEG), GROUP_NEG)


def meet_group(group, message, neg_ids, pos_cols, slot_cols, hidden_unit, units, shares, sums, targets):
    wide = neg_rows(message, group).astype(F32)
    scale = lax.rsqrt(row_sum(wide * wide) + EPSILON)
    unit = (wide * scale).astype(BF16)
    units[unit_rows(group), :] = unit
    logits = lax.dot_general(hidden_unit[...], unit, NT, preferred_element_type=F32)
    total = sums[...]
    for band in range(BANDS):
        keep = neg_ids[pl.ds(group * BANDS + band, 1), :] != pos_cols[...]
        near = logits[:, band * LANES : (band + 1) * LANES]
        grown = jnp.where(keep, jnp.exp2(near * (SHARPNESS * LOG2E)), 0.0)
        shares[share_rows(group, band), :] = grown
        total = total + grown
    sums[...] = total
    targets[...] += jnp.dot(
        pick(slot_cols, group),
        pos_rows(message, group).astype(BF16),
        preferred_element_type=F32,
    )


def settle(hidden_unit, sums, targets, loss, inverse):
    state = hidden_unit[...].astype(F32)
    wide = targets[...]
    scale = lax.rsqrt(row_sum(wide * wide) + EPSILON)
    unit = wide * scale
    logit = row_sum(state * unit) * SHARPNESS
    grown = jnp.exp(logit)
    total = grown + row_sum(sums[...])
    lost = jnp.broadcast_to(jnp.log(total) - logit, (TOKENS, LANES))
    for part in range(TOKENS // LANES):
        loss[pl.ds(part, 1), :] = lost[part * LANES : (part + 1) * LANES].T[:1]
    share = grown / total - 1.0
    inverse[...] = jnp.broadcast_to(1.0 / total, (TOKENS, LANES))
    upstream = (share * SHARPNESS) * state
    back = scale * (upstream - unit * row_sum(unit * upstream))
    targets[...] = (share * SHARPNESS) * unit
    return back.astype(BF16)


def return_group(group, message, slot_cols, hidden_unit, units, shares, inverse, d_pos, d_state, out):
    share = jnp.concatenate(
        [
            (shares[share_rows(group, band), :] * inverse[...]).astype(BF16)
            for band in range(BANDS)
        ],
        axis=1,
    )
    wide = neg_rows(message, group).astype(F32)
    scale = lax.rsqrt(row_sum(wide * wide) + EPSILON)
    unit = wide * scale
    upstream = (
        lax.dot_general(share, hidden_unit[...], TN, preferred_element_type=F32) * SHARPNESS
    )
    back = (scale * (upstream - unit * row_sum(unit * upstream))).astype(BF16)
    start = pl.multiple_of(group * GROUP, GROUP)
    for band in range(BANDS):
        out[pl.ds(start, GROUP), pl.ds(band * PER_OWNER, PER_OWNER), :] = back[
            :, band * LANES : (band + 1) * LANES
        ].reshape(GROUP, PER_OWNER, LANES)
    returned = lax.dot_general(pick(slot_cols, group), d_pos[...], TN, preferred_element_type=F32)
    parts = [
        returned[:, band * LANES : (band + 1) * LANES].reshape(GROUP, 1, CAPACITY, LANES)
        for band in range(BANDS)
    ]
    out[pl.ds(start, GROUP), pl.ds(NEG_LINES, CAPACITY * BANDS), :] = (
        jnp.concatenate(parts, axis=1).reshape(GROUP, CAPACITY * BANDS, LANES).astype(BF16)
    )
    d_state[...] += jnp.dot(share, units[unit_rows(group), :], preferred_element_type=F32)


def hidden_back(hidden, d_state, targets, grad):
    wide = hidden[...].astype(F32)
    scale = lax.rsqrt(row_sum(wide * wide) + EPSILON)
    unit = wide * scale
    upstream = d_state[...] * SHARPNESS + targets[...]
    grad[...] = (scale * (upstream - unit * row_sum(unit * upstream))).astype(BF16)


def pair_rows(message, group):
    parts = [neg_rows(message, group), neg_rows(message, group + 1)]
    parts += [pos_rows(message, at).astype(BF16) for at in (group, group + 1)]
    return jnp.concatenate(parts, axis=0)


def add_tile(start, count, neg_asked, pos_asked, group, rows):
    row = lax.broadcasted_iota(jnp.int32, (count, LANES), 0) + start

    def hits(asked, line):
        return jnp.where(row == asked[pl.ds(line, 1), :], 1.0, 0.0).astype(BF16)

    wide = [hits(neg_asked, group * BANDS + band) for band in range(2 * BANDS)]
    wide += [hits(pos_asked, group), hits(pos_asked, group + 1)]
    return jnp.dot(jnp.concatenate(wide, axis=1), rows, preferred_element_type=F32)


def add_pair(group, message, neg_asked, pos_asked, total):
    rows = pair_rows(message, group)

    def tile(index, _):
        start = pl.multiple_of(index * TILE, TILE)
        total[pl.ds(start, TILE), :] += add_tile(start, TILE, neg_asked, pos_asked, group, rows)
        return 0

    lax.fori_loop(0, ROWS // TILE, tile, 0)


def finish_kernel(before, message, neg_asked, pos_asked, loss_in, grad_in, total, loss, grad):
    index = pl.program_id(0)

    @pl.when(index == 0)
    def _():
        loss[...] = loss_in[...]
        grad[...] = grad_in[...]

    total[...] = before[...] + add_tile(
        index * END_TILE,
        END_TILE,
        neg_asked,
        pos_asked,
        GROUPS - 2,
        pair_rows(message, 0),
    )


SEQ_BITS = ("x0", "x1", "zl", "y0", "y1")
LOOP_BITS = ("c", "zh")
ITEM_FLIPS = (("y0", "zh", "c"), ("x0", "y1"), ("zl", "c"), ("x1", "zh"))
GROUP_FLIPS = ("c", "zh", "y1")


def own_bits():
    seq, loop = lax.axis_index("seq"), lax.axis_index("loop")
    bits = {name: lax.rem(lax.div(seq, 2**at), 2) for at, name in enumerate(SEQ_BITS)}
    bits.update({name: lax.rem(lax.div(loop, 2**at), 2) for at, name in enumerate(LOOP_BITS)})
    return bits


def partners(group):
    bits = own_bits()
    for at, name in enumerate(GROUP_FLIPS):
        turn = lax.rem(lax.div(group, 2**at), 2)
        bits[name] = bits[name] + turn - 2 * bits[name] * turn
    seq = sum(bits[name] * 2**at for at, name in enumerate(SEQ_BITS))
    loop = sum(bits[name] * 2**at for at, name in enumerate(LOOP_BITS))
    seq_turn = {name: (1 - 2 * bits[name]) * 2**at for at, name in enumerate(SEQ_BITS)}
    loop_turn = {name: (1 - 2 * bits[name]) * 2**at for at, name in enumerate(LOOP_BITS)}
    met = []
    for item in range(GROUP):
        flips = set()
        for at, names in enumerate(ITEM_FLIPS):
            if item >> at & 1:
                flips ^= set(names)
        met.append(
            (
                sum((seq_turn[name] for name in SEQ_BITS if name in flips), seq),
                sum((loop_turn[name] for name in LOOP_BITS if name in flips), loop),
            )
        )
    return met


def each_partner(act):
    def one(group, _):
        for item, device in enumerate(partners(group)):
            if item == 0:

                @pl.when(group > 0)
                def _():
                    act(group, item, device)

            else:
                act(group, item, device)
        return 0

    lax.fori_loop(0, GROUPS, one, 0)


def slot_of(owner):
    me = lax.axis_index("seq") * 4 + lax.axis_index("loop")
    apart = jnp.bitwise_xor(owner, me)
    names = LOOP_BITS + SEQ_BITS
    bit = {name: jnp.bitwise_and(jnp.right_shift(apart, at), 1) for at, name in enumerate(names)}
    first = jnp.bitwise_xor(jnp.bitwise_xor(bit["c"], bit["y0"]), bit["zl"])
    second = jnp.bitwise_xor(jnp.bitwise_xor(bit["zh"], bit["y0"]), bit["x1"])
    third = jnp.bitwise_xor(bit["y1"], bit["x0"])
    item = bit["y0"] + 2 * bit["x0"] + 4 * bit["zl"] + 8 * bit["x1"]
    return item + 16 * first + 32 * second + 64 * third


def columns_of(row, out):
    for part in range(TOKENS // LANES):
        square = jnp.broadcast_to(row[:, part * LANES : (part + 1) * LANES], (LANES, LANES))
        out[pl.ds(part * LANES, LANES), :] = square.T


def lanes_of(rows, out, count, skip):
    lane = lax.broadcasted_iota(jnp.int32, (GROUPS, LANES), 1)
    bands = count * GROUP // LANES
    share = LANES // count
    for band in range(bands):
        packed = jnp.zeros((GROUPS, LANES), jnp.int32)
        for part in range(share):
            some = rows[pl.ds(band * share + part, GROUPS, stride=GROUP), :]
            some = pltpu.roll(some, (part * count - skip) % LANES, axis=1)
            inside = (lane >= part * count) & (lane < (part + 1) * count)
            packed = jnp.where(inside, some, packed)
        out[pl.ds(band, GROUPS, stride=bands), :] = packed


def count_rows(flags):
    rows = flags.shape[0]
    while rows > 8:
        rows //= 2
        flags = flags[:rows] + flags[rows:]
    total = flags[:1]
    for row in range(1, 8):
        total = total + flags[row : row + 1]
    return total


def write_requests(negatives, pos_row, pos_cols, owned, met_ids, asks, slot_cols, rank_cols):
    lane = lax.broadcasted_iota(jnp.int32, (TOKENS, LANES), 1)
    line = lax.broadcasted_iota(jnp.int32, (TOKENS, LANES), 0)
    ids = pos_cols[...]
    slot = slot_of(jnp.right_shift(ids, 12))
    slot_row = slot_of(jnp.right_shift(pos_row[...], 12))
    ranks = []
    for part in range(TOKENS // LANES):
        near = slot_row[:, part * LANES : (part + 1) * LANES]
        earlier = (slot == near) & (line < lane + part * LANES)
        ranks.append(count_rows(jnp.where(earlier, 1, 0)))
    columns_of(jnp.concatenate(ranks, axis=1), rank_cols)
    rank = rank_cols[...]
    slot_cols[...] = slot * CAPACITY + rank
    named = jnp.where(slot == lane, jnp.bitwise_and(ids, ROWS - 1) + 1, 0)
    wanted = [jnp.zeros((PER_OWNER, LANES), jnp.int32)]
    for place in range(CAPACITY):
        wanted.append(count_rows(jnp.where(rank == place, named, 0)))
    wanted.append(jnp.zeros((LANES - ASKED, LANES), jnp.int32))
    wanted = jnp.concatenate(wanted, axis=0).T - 1
    share = LANES // PER_OWNER
    for part in range(share):
        owned[pl.ds(part, DEVICES // share, stride=share), :] = pltpu.roll(
            negatives[...], (LANES - part * PER_OWNER) % LANES, axis=1
        )

    def order(group, _):
        for item, (seq, loop) in enumerate(partners(group)):
            met_ids[pl.ds(group * GROUP + item, 1), :] = owned[pl.ds(seq * 4 + loop, 1), :]
        return 0

    lax.fori_loop(0, GROUPS, order, 0)
    slots = lax.broadcasted_iota(jnp.int32, (DEVICES, LANES), 1)
    asks[...] = jnp.where(
        slots < PER_OWNER, jnp.bitwise_and(met_ids[...], ROWS - 1), wanted
    )


def step_kernel(
    events_in,
    carried_in,
    stamp_row,
    negatives,
    pos_row,
    in_gain,
    w_in_in,
    attn_gain,
    w_out_in,
    table,
    loss_out,
    grad_out,
    total_out,
    last,
    neg_asked_out,
    pos_asked_out,
    events,
    carried,
    w_in,
    w_out,
    far,
    stamp_cols,
    pos_cols,
    slot_cols,
    rank_cols,
    owned,
    met_ids,
    asks,
    asked,
    asked_scalar,
    neg_ids,
    neg_asked,
    pos_asked,
    lines,
    units,
    stage,
    sent,
    answered,
    returned,
    gate,
    queries,
    keys,
    values,
    mixed,
    hidden,
    hidden_unit,
    sums,
    targets,
    inverse,
    d_pos,
    d_state,
    loss,
    grad,
    total,
    load_sems,
    local_sem,
    ask_send,
    ask_recv,
    halo_send,
    halo_recv,
    row_send,
    row_recv,
    back_send,
    back_recv,
    out_sems,
):
    seq, loop = lax.axis_index("seq"), lax.axis_index("loop")
    barrier = pltpu.get_barrier_semaphore()
    each_partner(
        lambda group, item, device: pl.semaphore_signal(
            barrier, inc=1, device_id=device, device_id_type=pl.DeviceIdType.MESH
        )
    )
    loads = [
        pltpu.make_async_copy(source, target, load_sems.at[at])
        for at, (source, target) in enumerate(
            [
                (events_in, events),
                (table, units),
                (w_in_in, w_in),
                (w_out_in, w_out),
                (carried_in, carried),
            ]
        )
    ]
    for load in loads:
        load.start()

    def to_partner(source, target, send, recv, device):
        return pltpu.make_async_remote_copy(
            src_ref=source,
            dst_ref=target,
            send_sem=send,
            recv_sem=recv,
            device_id=device,
            device_id_type=pl.DeviceIdType.MESH,
        )

    other = (seq, loop + 1 - 2 * lax.rem(loop, 2))

    def expect(buffer, send, recv):
        return to_partner(buffer, buffer, send, recv, other)

    columns_of(pos_row, pos_cols)
    columns_of(stamp_row, stamp_cols)
    write_requests(
        negatives, pos_row, pos_cols, owned, met_ids, asks, slot_cols, rank_cols
    )
    asked[pl.ds(0, 1), :] = asks[pl.ds(0, 1), :]
    loads[0].wait()
    pl.semaphore_wait(barrier, DEVICES - 1)

    each_partner(
        lambda group, item, device: to_partner(
            asks.at[pl.ds(group * GROUP + item, 1)],
            asked.at[pl.ds(group * GROUP + item, 1)],
            ask_send,
            ask_recv.at[group],
            device,
        ).start()
    )
    place = lax.rem(seq, 4)
    quarter = TOKENS // 4

    def shifted(steps):
        return (lax.rem(seq + 32 + steps, 32), loop)

    def halo(at, source, target, device):
        return to_partner(source, target, halo_send.at[at], halo_recv.at[at], device)

    def piece(source, part, device):
        rows = pl.ds(part * quarter, quarter)
        return halo(1, far.at[source, rows], far.at[1, rows], device)

    near_halos = [
        (place < 3, halo(0, events, far.at[0], shifted(1))),
        (place == 3, halo(3, events, far.at[3], shifted(4))),
        (place < 4, halo(2, events, far.at[2], shifted(3))),
    ]
    corner = [(place == 3, halo(0, far.at[3], far.at[0], shifted(-3)))]
    forward = [
        (place < 4, piece(0, 0, shifted(1))),
        (place < 3, piece(0, 1, shifted(1))),
        (place == 2, piece(0, 2, shifted(1))),
    ]
    backward = [
        (place == 1, piece(2, 1, shifted(-1))),
        (place > 0, piece(2, 2, shifted(-1))),
        (place < 4, piece(2, 3, shifted(-1))),
    ]

    def start_all(copies):
        for when, copy in copies:
            pl.when(when)(copy.start)

    def await_halo(at):
        halo(at, far.at[at], far.at[at], other).wait_recv()

    start_all(near_halos)

    lanes_of(met_ids, neg_ids, PER_OWNER, 0)
    loads[1].wait()
    widen_table(units, lines)
    def send_group(group, target, base, send, recv):
        for item, device in enumerate(partners(group)):

            def start(item=item, device=device):
                to_partner(
                    sent.at[group * GROUP + item],
                    target.at[(group - base) * GROUP + item],
                    send,
                    recv.at[group],
                    device,
                ).start()

            if item == 0:
                pl.when(group > 0)(start)
            else:
                start()

    def keep_own(target):
        mine = pltpu.make_async_copy(sent.at[0], target.at[0], local_sem)
        mine.start()
        mine.wait()

    def await_group(group, target, send, recv):
        @pl.when(group == 0)
        def _():
            expect(target.at[pl.ds(1, GROUP - 1)], send, recv.at[0]).wait_recv()

        @pl.when(group > 0)
        def _():
            expect(target.at[pl.ds(0, GROUP)], send, recv.at[group]).wait_recv()

    def answer_group(group, _):
        start = pl.multiple_of(group * GROUP, GROUP)
        await_group(group, asked, ask_send, ask_recv)
        scalars = pltpu.make_async_copy(
            asked.at[pl.ds(start, GROUP)], asked_scalar.at[pl.ds(start, GROUP)], local_sem
        )
        scalars.start()
        scalars.wait()

        def one(item, _):
            answer(asked_scalar, lines, stage, sent, group * GROUP + item)
            return 0

        lax.fori_loop(0, GROUP, one, 0)
        send_group(group, answered, 0, row_send, row_recv)
        @pl.when(group == CORNER_TURN)
        def _():
            pl.when(place == 3)(functools.partial(await_halo, 3))
            start_all(corner)

        @pl.when(group == BACK_TURN)
        def _():
            await_halo(2)
            start_all(backward)

        @pl.when(group == FORWARD_TURN)
        def _():
            await_halo(0)
            start_all(forward)

        return 0

    lax.fori_loop(0, GROUPS, answer_group, 0)
    keep_own(answered)
    loads[2].wait()
    project_own(events, in_gain, w_in, gate, queries, keys, values)
    sums[...] = jnp.zeros_like(sums)
    targets[...] = jnp.zeros_like(targets)
    d_state[...] = jnp.zeros_like(d_state)
    lanes_of(asked, neg_asked, PER_OWNER, 0)
    lanes_of(asked, pos_asked, CAPACITY, PER_OWNER)
    await_halo(1)

    def far_block(reach, _):
        live = jnp.where(seq >= reach, 1.0, 0.0).astype(F32)
        project_far(reach, far[reach - 1], live, in_gain, w_in, keys, values)
        return 0

    lax.fori_loop(1, WINDOW, far_block, 0)
    attend(stamp_cols, stamp_row, queries, keys, values, mixed)
    loads[3].wait()
    loads[4].wait()
    finish_hidden(events, carried, attn_gain, w_out, gate, mixed, hidden)
    unit_hidden(hidden, hidden_unit)

    def meet(group, _):
        await_group(group, answered, row_send, row_recv)
        meet_group(
            group, answered, neg_ids, pos_cols, slot_cols, hidden_unit, units, lines, sums, targets
        )
        return 0

    lax.fori_loop(0, GROUPS, meet, 0)
    d_pos[...] = settle(hidden_unit, sums, targets, loss, inverse)
    expect(sent.at[pl.ds(0, DEVICES - 1)], row_send, row_recv.at[0]).wait_send()

    def back(group, _):
        return_group(
            group, answered, slot_cols, hidden_unit, units, lines, inverse, d_pos, d_state, sent
        )
        send_group(group, returned, 0, back_send, back_recv)
        return 0

    lax.fori_loop(0, GROUPS - 2, back, 0)

    def back_last(group, _):
        return_group(
            group, answered, slot_cols, hidden_unit, units, lines, inverse, d_pos, d_state, sent
        )
        send_group(group, last, GROUPS - 2, back_send, back_recv)
        return 0

    lax.fori_loop(GROUPS - 2, GROUPS, back_last, 0)
    keep_own(returned)
    hidden_back(hidden, d_state, targets, grad)
    total[...] = jnp.zeros_like(total)

    def collect(pair, _):
        await_group(2 * pair, returned, back_send, back_recv)
        await_group(2 * pair + 1, returned, back_send, back_recv)
        add_pair(2 * pair, returned, neg_asked, pos_asked, total)
        return 0

    lax.fori_loop(0, GROUPS // 2 - 1, collect, 0)
    outs = [
        pltpu.make_async_copy(source, target, out_sems.at[at])
        for at, (source, target) in enumerate(
            [
                (total, total_out),
                (loss, loss_out),
                (grad, grad_out),
                (neg_asked, neg_asked_out),
                (pos_asked, pos_asked_out),
            ]
        )
    ]
    for out in outs:
        out.start()
    expect(asked.at[pl.ds(1, DEVICES - 1)], ask_send, ask_recv.at[0]).wait_send()
    for when, copy in near_halos + corner + forward + backward:
        pl.when(when)(copy.wait_send)
    expect(sent.at[pl.ds(0, DEVICES - 1)], back_send, back_recv.at[0]).wait_send()
    for out in outs:
        out.wait()
    for end in range(2):
        expect(
            last.at[pl.ds(end * GROUP, GROUP)], back_send, back_recv.at[GROUPS - 2 + end]
        ).wait_recv()


def whole(kind, shape):
    return pltpu.VMEM(shape, kind)


def on_device(events, carried, positions, neg_ids, pos_ids, in_gain, w_in, attn_gain, w_out, table):
    inside = pl.BlockSpec(memory_space=pltpu.VMEM)
    outside = pl.BlockSpec(memory_space=pl.ANY)
    integers = jnp.int32
    loss, grad_hidden, most, last, neg_asked, pos_asked = pl.pallas_call(
        step_kernel,
        out_shape=(
            jax.ShapeDtypeStruct((TOKENS // LANES, LANES), F32),
            jax.ShapeDtypeStruct((TOKENS, WIDTH), BF16),
            jax.ShapeDtypeStruct((ROWS, WIDTH), F32),
            jax.ShapeDtypeStruct((2 * GROUP, MESSAGE, LANES), BF16),
            jax.ShapeDtypeStruct((GROUPS * BANDS, LANES), integers),
            jax.ShapeDtypeStruct((GROUPS, LANES), integers),
        ),
        in_specs=[
            outside,
            outside,
            inside,
            inside,
            inside,
            inside,
            outside,
            inside,
            outside,
            outside,
        ],
        out_specs=(outside,) * 6,
        scratch_shapes=[
            whole(BF16, (TOKENS, WIDTH)),
            whole(F32, (TOKENS, WIDTH)),
            whole(BF16, (WIDTH, 4 * WIDTH)),
            whole(BF16, (WIDTH, WIDTH)),
            whole(BF16, (WINDOW, TOKENS, WIDTH)),
            whole(integers, (TOKENS, LANES)),
            whole(integers, (TOKENS, LANES)),
            whole(integers, (TOKENS, LANES)),
            whole(integers, (TOKENS, LANES)),
            whole(integers, (DEVICES, LANES)),
            whole(integers, (DEVICES, LANES)),
            whole(integers, (DEVICES, LANES)),
            whole(integers, (DEVICES, LANES)),
            pltpu.SMEM((DEVICES, LANES), integers),
            whole(integers, (GROUPS * BANDS, LANES)),
            whole(integers, (GROUPS * BANDS, LANES)),
            whole(integers, (GROUPS, LANES)),
            whole(F32, (ROWS * BANDS, LANES)),
            whole(BF16, (ROWS, WIDTH)),
            whole(F32, (MESSAGE, LANES)),
            whole(BF16, (DEVICES, MESSAGE, LANES)),
            whole(BF16, (DEVICES, MESSAGE, LANES)),
            whole(BF16, (DEVICES - 2 * GROUP, MESSAGE, LANES)),
            whole(BF16, (TOKENS, WIDTH)),
            whole(BF16, (BANDS, TOKENS, LANES)),
            whole(BF16, (WINDOW, BANDS, TOKENS, LANES)),
            whole(BF16, (WINDOW, BANDS, TOKENS, LANES)),
            whole(F32, (BANDS, TOKENS, LANES)),
            whole(BF16, (TOKENS, WIDTH)),
            whole(BF16, (TOKENS, WIDTH)),
            whole(F32, (TOKENS, LANES)),
            whole(F32, (TOKENS, WIDTH)),
            whole(F32, (TOKENS, LANES)),
            whole(BF16, (TOKENS, WIDTH)),
            whole(F32, (TOKENS, WIDTH)),
            whole(F32, (TOKENS // LANES, LANES)),
            whole(BF16, (TOKENS, WIDTH)),
            whole(F32, (ROWS, WIDTH)),
            pltpu.SemaphoreType.DMA((5,)),
            pltpu.SemaphoreType.DMA,
            pltpu.SemaphoreType.DMA,
            pltpu.SemaphoreType.DMA((GROUPS,)),
            pltpu.SemaphoreType.DMA((4,)),
            pltpu.SemaphoreType.DMA((4,)),
            pltpu.SemaphoreType.DMA,
            pltpu.SemaphoreType.DMA((GROUPS,)),
            pltpu.SemaphoreType.DMA,
            pltpu.SemaphoreType.DMA((GROUPS,)),
            pltpu.SemaphoreType.DMA((5,)),
        ],
        compiler_params=pltpu.CompilerParams(
            collective_id=0, has_side_effects=True, vmem_limit_bytes=BANK
        ),
        name="step",
    )(
        events[0],
        carried[0],
        positions,
        neg_ids.reshape(NEG // LANES, LANES),
        pos_ids,
        in_gain[None, :],
        w_in,
        attn_gain[None, :],
        w_out,
        table,
    )
    fixed = [most, last, neg_asked, pos_asked, loss, grad_hidden]
    tile = pl.BlockSpec((END_TILE, WIDTH), lambda index: (index, 0))
    rest = [
        pl.BlockSpec(array.shape, lambda index, rank=array.ndim: (0,) * rank) for array in fixed[1:]
    ]
    grad_table, loss, grad_hidden = pl.pallas_call(
        finish_kernel,
        grid=(ROWS // END_TILE,),
        out_shape=(
            jax.ShapeDtypeStruct((ROWS, WIDTH), F32),
            jax.ShapeDtypeStruct(loss.shape, F32),
            jax.ShapeDtypeStruct(grad_hidden.shape, BF16),
        ),
        in_specs=[tile] + rest,
        out_specs=(tile, rest[3], rest[4]),
        compiler_params=pltpu.CompilerParams(vmem_limit_bytes=BANK),
        name="finish",
    )(*fixed)
    return (loss.reshape(1, TOKENS), grad_hidden[None], grad_table)


def solution(mesh):
    return jax.shard_map(
        on_device,
        mesh=mesh,
        in_specs=(
            P("loop", "seq", None),
            P("loop", "seq", None),
            P("loop", "seq"),
            P("loop", "seq", None),
            P("loop", "seq"),
            P(),
            P(),
            P(),
            P(),
            P(("seq", "loop"), None),
        ),
        out_specs=(P("loop", "seq"), P("loop", "seq", None), P(("seq", "loop"), None)),
        check_vma=False,
    )
```

```python
import functools

import jax
import jax.numpy as jnp
from jax import lax
from jax.experimental import pallas as pl
from jax.experimental.pallas import tpu as pltpu
from jax.sharding import PartitionSpec as P

HEADS = 8
DH = 64
WINDOW = 4
WIDTH = HEADS * DH
LANES = 128
BANDS = WIDTH // LANES
TOKENS = 512
NEG = 4096
ROWS = 4096
DEVICES = 128
PER_OWNER = NEG // DEVICES
CAPACITY = 2 * TOKENS // DEVICES
ASKED = PER_OWNER + CAPACITY
MESSAGE = ASKED * BANDS
GROUP = 16
GROUPS = DEVICES // GROUP
GROUP_NEG = GROUP * PER_OWNER
GROUP_POS = GROUP * CAPACITY
NEG_LINES = PER_OWNER * BANDS

SHARPNESS = 50.0
LOG2E = 1.4426950408889634
EPSILON = 1e-06
F32 = jnp.float32
BF16 = jnp.bfloat16
NT = (((1,), (1,)), ((), ()))
TN = (((0,), (0,)), ((), ()))
TILE = 1024
END_TILE = 512
CORNER_TURN, BACK_TURN, FORWARD_TURN = 3, 4, 5
BANK = 62 * 2**20


def silu(value):
    half = value * 0.5
    return half + half * jnp.tanh(half)


def row_sum(value):
    return jnp.sum(value, axis=-1, keepdims=True)


def normalise(rows, gain):
    wide = rows.astype(F32)
    scale = lax.rsqrt(row_sum(wide * wide) * (1.0 / WIDTH) + EPSILON)
    return (wide * scale * gain).astype(BF16)


def store_bands(ref, lead, value):
    for band in range(BANDS):
        ref[lead + (band,)] = value[:, band * LANES : (band + 1) * LANES]


def project_own(events, gain, w_in, gate, queries, keys, values):
    normed = normalise(events[...], gain[...])

    def column(index):
        part = jnp.dot(
            normed, w_in[:, index * WIDTH : (index + 1) * WIDTH], preferred_element_type=F32
        )
        return silu(part).astype(BF16)

    gate[...] = column(0)
    store_bands(values, (0,), column(1))
    store_bands(queries, (), (column(2).astype(F32) * 0.0625).astype(BF16))
    store_bands(keys, (0,), column(3))


def project_far(reach, rows, live, gain, w_in, keys, values):
    normed = normalise(rows, gain[...])

    def column(index):
        part = jnp.dot(
            normed, w_in[:, index * WIDTH : (index + 1) * WIDTH], preferred_element_type=F32
        )
        return (silu(part) * live).astype(BF16)

    store_bands(values, (reach,), column(1))
    store_bands(keys, (reach,), column(3))


def attend(stamp_cols, stamp_row, queries, keys, values, mixed):
    allowed = stamp_row[...] <= stamp_cols[:, :1]
    first = lax.broadcasted_iota(jnp.int32, (TOKENS, LANES), 1) < DH

    def pair(band, _):
        both = queries[band].astype(F32)
        parts = [
            jnp.where(first, both, 0.0).astype(BF16),
            jnp.where(first, 0.0, both).astype(BF16),
        ]

        def block(index, own):
            outs = []
            for part in parts:
                half = lax.dot_general(part, keys[index, band], NT, preferred_element_type=F32)
                weight = half + half * jnp.tanh(half)
                if own:
                    weight = jnp.where(allowed, weight, 0.0)
                outs.append(
                    jnp.dot(weight.astype(BF16), values[index, band], preferred_element_type=F32)
                )
            return jnp.where(first, outs[0], outs[1])

        mixed[band] = block(0, True)

        def later(index, _):
            mixed[band] += block(index, False)
            return 0

        lax.fori_loop(1, WINDOW, later, 0)
        return 0

    lax.fori_loop(0, BANDS, pair, 0)


def finish_hidden(events, carried, gain, w_out, gate, mixed, hidden):
    parts = [
        carried[:, band * LANES : (band + 1) * LANES] + mixed[band] for band in range(BANDS)
    ]
    squares = sum(row_sum(part * part) for part in parts)
    scale = lax.rsqrt(squares * (1.0 / WIDTH) + EPSILON)
    attended = jnp.concatenate(parts, axis=1)
    gated = (attended * scale * gain[...] * gate[...].astype(F32)).astype(BF16)
    hidden[...] = (
        events[...].astype(F32) + jnp.dot(gated, w_out[...], preferred_element_type=F32)
    ).astype(BF16)


def widen_table(table, lines):
    step = 256

    def part(index, _):
        start = pl.multiple_of(index * step, step)
        rows = table[pl.ds(start, step), :].astype(F32)
        for band in range(BANDS):
            lines[pl.ds(start * BANDS + band, step, stride=BANDS), :] = rows[
                :, band * LANES : (band + 1) * LANES
            ]
        return 0

    lax.fori_loop(0, ROWS // step, part, 0)


def answer(asked, lines, stage, message, peer):
    for slot in range(ASKED):
        row = jnp.maximum(asked[peer, slot], 0)
        stage[pl.ds(slot * BANDS, BANDS), :] = lines[pl.ds(row * BANDS, BANDS), :]
    for band in range(BANDS):
        message[peer, pl.ds(band * PER_OWNER, PER_OWNER), :] = stage[
            pl.ds(band, PER_OWNER, stride=BANDS), :
        ].astype(BF16)
    tail = [
        stage[pl.ds(NEG_LINES + band, CAPACITY, stride=BANDS), :] for band in range(BANDS)
    ]
    message[peer, pl.ds(NEG_LINES, CAPACITY * BANDS), :] = jnp.concatenate(tail, axis=0).astype(
        BF16
    )


def neg_rows(message, group):
    start = pl.multiple_of(group * GROUP, GROUP)
    parts = [
        message[pl.ds(start, GROUP), pl.ds(band * PER_OWNER, PER_OWNER), :].reshape(
            GROUP_NEG, LANES
        )
        for band in range(BANDS)
    ]
    return jnp.concatenate(parts, axis=1)


def pos_rows(message, group):
    start = pl.multiple_of(group * GROUP, GROUP)
    block = message[pl.ds(start, GROUP), pl.ds(NEG_LINES, CAPACITY * BANDS), :].astype(F32)
    block = block.reshape(GROUP, BANDS, CAPACITY, LANES)
    parts = [block[:, band].reshape(GROUP_POS, LANES) for band in range(BANDS)]
    return jnp.concatenate(parts, axis=1)


def unit_hidden(hidden, hidden_unit):
    wide = hidden[...].astype(F32)
    scale = lax.rsqrt(row_sum(wide * wide) + EPSILON)
    hidden_unit[...] = (wide * scale).astype(BF16)


def pick(slot_cols, group):
    lane = lax.broadcasted_iota(jnp.int32, (TOKENS, GROUP_POS), 1) + group * GROUP_POS
    return jnp.where(slot_cols[...] == lane, 1.0, 0.0).astype(BF16)


def share_rows(group, band):
    return pl.ds(pl.multiple_of((group * BANDS + band) * TOKENS, TOKENS), TOKENS)


def unit_rows(group):
    return pl.ds(pl.multiple_of(group * GROUP_NEG, GROUP_NEG), GROUP_NEG)


def meet_group(group, message, neg_ids, pos_cols, slot_cols, hidden_unit, units, shares, sums, targets):
    wide = neg_rows(message, group).astype(F32)
    scale = lax.rsqrt(row_sum(wide * wide) + EPSILON)
    unit = (wide * scale).astype(BF16)
    units[unit_rows(group), :] = unit
    logits = lax.dot_general(hidden_unit[...], unit, NT, preferred_element_type=F32)
    total = sums[...]
    for band in range(BANDS):
        keep = neg_ids[pl.ds(group * BANDS + band, 1), :] != pos_cols[...]
        near = logits[:, band * LANES : (band + 1) * LANES]
        grown = jnp.where(keep, jnp.exp2(near * (SHARPNESS * LOG2E)), 0.0)
        shares[share_rows(group, band), :] = grown
        total = total + grown
    sums[...] = total
    targets[...] += jnp.dot(
        pick(slot_cols, group),
        pos_rows(message, group).astype(BF16),
        preferred_element_type=F32,
    )


def settle(hidden_unit, sums, targets, loss, inverse):
    state = hidden_unit[...].astype(F32)
    wide = targets[...]
    scale = lax.rsqrt(row_sum(wide * wide) + EPSILON)
    unit = wide * scale
    logit = row_sum(state * unit) * SHARPNESS
    grown = jnp.exp(logit)
    total = grown + row_sum(sums[...])
    lost = jnp.broadcast_to(jnp.log(total) - logit, (TOKENS, LANES))
    for part in range(TOKENS // LANES):
        loss[pl.ds(part, 1), :] = lost[part * LANES : (part + 1) * LANES].T[:1]
    share = grown / total - 1.0
    inverse[...] = jnp.broadcast_to(1.0 / total, (TOKENS, LANES))
    upstream = (share * SHARPNESS) * state
    back = scale * (upstream - unit * row_sum(unit * upstream))
    targets[...] = (share * SHARPNESS) * unit
    return back.astype(BF16)


def return_group(group, message, slot_cols, hidden_unit, units, shares, inverse, d_pos, d_state, out):
    share = jnp.concatenate(
        [
            (shares[share_rows(group, band), :] * inverse[...]).astype(BF16)
            for band in range(BANDS)
        ],
        axis=1,
    )
    wide = neg_rows(message, group).astype(F32)
    scale = lax.rsqrt(row_sum(wide * wide) + EPSILON)
    unit = wide * scale
    upstream = (
        lax.dot_general(share, hidden_unit[...], TN, preferred_element_type=F32) * SHARPNESS
    )
    back = (scale * (upstream - unit * row_sum(unit * upstream))).astype(BF16)
    start = pl.multiple_of(group * GROUP, GROUP)
    for band in range(BANDS):
        out[pl.ds(start, GROUP), pl.ds(band * PER_OWNER, PER_OWNER), :] = back[
            :, band * LANES : (band + 1) * LANES
        ].reshape(GROUP, PER_OWNER, LANES)
    returned = lax.dot_general(pick(slot_cols, group), d_pos[...], TN, preferred_element_type=F32)
    parts = [
        returned[:, band * LANES : (band + 1) * LANES].reshape(GROUP, 1, CAPACITY, LANES)
        for band in range(BANDS)
    ]
    out[pl.ds(start, GROUP), pl.ds(NEG_LINES, CAPACITY * BANDS), :] = (
        jnp.concatenate(parts, axis=1).reshape(GROUP, CAPACITY * BANDS, LANES).astype(BF16)
    )
    d_state[...] += jnp.dot(share, units[unit_rows(group), :], preferred_element_type=F32)


def hidden_back(hidden, d_state, targets, grad):
    wide = hidden[...].astype(F32)
    scale = lax.rsqrt(row_sum(wide * wide) + EPSILON)
    unit = wide * scale
    upstream = d_state[...] * SHARPNESS + targets[...]
    grad[...] = (scale * (upstream - unit * row_sum(unit * upstream))).astype(BF16)


def group_rows(message, groups):
    parts = [neg_rows(message, group) for group in groups]
    parts += [pos_rows(message, group).astype(BF16) for group in groups]
    return jnp.concatenate(parts, axis=0)


def add_tile(start, count, neg_asked, pos_asked, groups, rows):
    row = lax.broadcasted_iota(jnp.int32, (count, LANES), 0) + start

    def hits(asked, line):
        return jnp.where(row == asked[pl.ds(line, 1), :], 1.0, 0.0).astype(BF16)

    wide = [
        hits(neg_asked, group * BANDS + band) for group in groups for band in range(BANDS)
    ]
    wide += [hits(pos_asked, group) for group in groups]
    return jnp.dot(jnp.concatenate(wide, axis=1), rows, preferred_element_type=F32)


def add_groups(groups, message, neg_asked, pos_asked, total):
    rows = group_rows(message, groups)

    def tile(index, _):
        start = pl.multiple_of(index * TILE, TILE)
        total[pl.ds(start, TILE), :] += add_tile(start, TILE, neg_asked, pos_asked, groups, rows)
        return 0

    lax.fori_loop(0, ROWS // TILE, tile, 0)


def finish_kernel(before, message, neg_asked, pos_asked, loss_in, grad_in, total, loss, grad):
    index = pl.program_id(0)

    @pl.when(index == 0)
    def _():
        loss[...] = loss_in[...]
        grad[...] = grad_in[...]

    start = pl.multiple_of(index * END_TILE, END_TILE)
    total[...] = before[pl.ds(start, END_TILE), :] + add_tile(
        start,
        END_TILE,
        neg_asked,
        pos_asked,
        [GROUPS - 1],
        group_rows(message, [0]),
    )


SEQ_BITS = ("x0", "x1", "zl", "y0", "y1")
LOOP_BITS = ("c", "zh")
ITEM_FLIPS = (("y0", "zh", "c"), ("x0", "y1"), ("zl", "c"), ("x1", "zh"))
GROUP_FLIPS = ("c", "zh", "y1")


def own_bits():
    seq, loop = lax.axis_index("seq"), lax.axis_index("loop")
    bits = {name: lax.rem(lax.div(seq, 2**at), 2) for at, name in enumerate(SEQ_BITS)}
    bits.update({name: lax.rem(lax.div(loop, 2**at), 2) for at, name in enumerate(LOOP_BITS)})
    return bits


def partners(group):
    bits = own_bits()
    for at, name in enumerate(GROUP_FLIPS):
        turn = lax.rem(lax.div(group, 2**at), 2)
        bits[name] = bits[name] + turn - 2 * bits[name] * turn
    seq = sum(bits[name] * 2**at for at, name in enumerate(SEQ_BITS))
    loop = sum(bits[name] * 2**at for at, name in enumerate(LOOP_BITS))
    seq_turn = {name: (1 - 2 * bits[name]) * 2**at for at, name in enumerate(SEQ_BITS)}
    loop_turn = {name: (1 - 2 * bits[name]) * 2**at for at, name in enumerate(LOOP_BITS)}
    met = []
    for item in range(GROUP):
        flips = set()
        for at, names in enumerate(ITEM_FLIPS):
            if item >> at & 1:
                flips ^= set(names)
        met.append(
            (
                sum((seq_turn[name] for name in SEQ_BITS if name in flips), seq),
                sum((loop_turn[name] for name in LOOP_BITS if name in flips), loop),
            )
        )
    return met


def each_partner(act):
    def one(group, _):
        for item, device in enumerate(partners(group)):
            if item == 0:

                @pl.when(group > 0)
                def _():
                    act(group, item, device)

            else:
                act(group, item, device)
        return 0

    lax.fori_loop(0, GROUPS, one, 0)


def slot_of(owner):
    me = lax.axis_index("seq") * 4 + lax.axis_index("loop")
    apart = jnp.bitwise_xor(owner, me)
    names = LOOP_BITS + SEQ_BITS
    bit = {name: jnp.bitwise_and(jnp.right_shift(apart, at), 1) for at, name in enumerate(names)}
    first = jnp.bitwise_xor(jnp.bitwise_xor(bit["c"], bit["y0"]), bit["zl"])
    second = jnp.bitwise_xor(jnp.bitwise_xor(bit["zh"], bit["y0"]), bit["x1"])
    third = jnp.bitwise_xor(bit["y1"], bit["x0"])
    item = bit["y0"] + 2 * bit["x0"] + 4 * bit["zl"] + 8 * bit["x1"]
    return item + 16 * first + 32 * second + 64 * third


def columns_of(row, out):
    for part in range(TOKENS // LANES):
        square = jnp.broadcast_to(row[:, part * LANES : (part + 1) * LANES], (LANES, LANES))
        out[pl.ds(part * LANES, LANES), :] = square.T


def lanes_of(rows, out, count, skip):
    lane = lax.broadcasted_iota(jnp.int32, (GROUPS, LANES), 1)
    bands = count * GROUP // LANES
    share = LANES // count
    for band in range(bands):
        packed = jnp.zeros((GROUPS, LANES), jnp.int32)
        for part in range(share):
            some = rows[pl.ds(band * share + part, GROUPS, stride=GROUP), :]
            some = pltpu.roll(some, (part * count - skip) % LANES, axis=1)
            inside = (lane >= part * count) & (lane < (part + 1) * count)
            packed = jnp.where(inside, some, packed)
        out[pl.ds(band, GROUPS, stride=bands), :] = packed


def count_rows(flags):
    rows = flags.shape[0]
    while rows > 8:
        rows //= 2
        flags = flags[:rows] + flags[rows:]
    total = flags[:1]
    for row in range(1, 8):
        total = total + flags[row : row + 1]
    return total


def write_requests(negatives, pos_row, pos_cols, owned, met_ids, asks, slot_cols, rank_cols):
    lane = lax.broadcasted_iota(jnp.int32, (TOKENS, LANES), 1)
    line = lax.broadcasted_iota(jnp.int32, (TOKENS, LANES), 0)
    ids = pos_cols[...]
    slot = slot_of(jnp.right_shift(ids, 12))
    slot_row = slot_of(jnp.right_shift(pos_row[...], 12))
    ranks = []
    for part in range(TOKENS // LANES):
        near = slot_row[:, part * LANES : (part + 1) * LANES]
        earlier = (slot == near) & (line < lane + part * LANES)
        ranks.append(count_rows(jnp.where(earlier, 1, 0)))
    columns_of(jnp.concatenate(ranks, axis=1), rank_cols)
    rank = rank_cols[...]
    slot_cols[...] = slot * CAPACITY + rank
    named = jnp.where(slot == lane, jnp.bitwise_and(ids, ROWS - 1) + 1, 0)
    wanted = [jnp.zeros((PER_OWNER, LANES), jnp.int32)]
    for place in range(CAPACITY):
        wanted.append(count_rows(jnp.where(rank == place, named, 0)))
    wanted.append(jnp.zeros((LANES - ASKED, LANES), jnp.int32))
    wanted = jnp.concatenate(wanted, axis=0).T - 1
    share = LANES // PER_OWNER
    for part in range(share):
        owned[pl.ds(part, DEVICES // share, stride=share), :] = pltpu.roll(
            negatives[...], (LANES - part * PER_OWNER) % LANES, axis=1
        )

    def order(group, _):
        for item, (seq, loop) in enumerate(partners(group)):
            met_ids[pl.ds(group * GROUP + item, 1), :] = owned[pl.ds(seq * 4 + loop, 1), :]
        return 0

    lax.fori_loop(0, GROUPS, order, 0)
    slots = lax.broadcasted_iota(jnp.int32, (DEVICES, LANES), 1)
    asks[...] = jnp.where(
        slots < PER_OWNER, jnp.bitwise_and(met_ids[...], ROWS - 1), wanted
    )


def step_kernel(
    events_in,
    carried_in,
    stamp_row,
    negatives,
    pos_row,
    in_gain,
    w_in_in,
    attn_gain,
    w_out_in,
    table,
    loss,
    grad,
    total,
    last,
    neg_asked,
    pos_asked,
    events,
    carried,
    w_in,
    w_out,
    far,
    stamp_cols,
    pos_cols,
    slot_cols,
    rank_cols,
    owned,
    met_ids,
    asks,
    asked,
    asked_scalar,
    neg_ids,
    lines,
    units,
    stage,
    sent,
    answered,
    returned,
    gate,
    queries,
    keys,
    values,
    mixed,
    hidden,
    hidden_unit,
    sums,
    targets,
    inverse,
    d_pos,
    d_state,
    load_sems,
    local_sem,
    ask_send,
    ask_recv,
    halo_send,
    halo_recv,
    row_send,
    row_recv,
    back_send,
    back_recv,
):
    seq, loop = lax.axis_index("seq"), lax.axis_index("loop")
    barrier = pltpu.get_barrier_semaphore()
    each_partner(
        lambda group, item, device: pl.semaphore_signal(
            barrier, inc=1, device_id=device, device_id_type=pl.DeviceIdType.MESH
        )
    )
    loads = [
        pltpu.make_async_copy(source, target, load_sems.at[at])
        for at, (source, target) in enumerate(
            [
                (events_in, events),
                (table, units),
                (w_in_in, w_in),
                (w_out_in, w_out),
                (carried_in, carried),
            ]
        )
    ]
    for load in loads:
        load.start()

    def to_partner(source, target, send, recv, device):
        return pltpu.make_async_remote_copy(
            src_ref=source,
            dst_ref=target,
            send_sem=send,
            recv_sem=recv,
            device_id=device,
            device_id_type=pl.DeviceIdType.MESH,
        )

    other = (seq, loop + 1 - 2 * lax.rem(loop, 2))

    def expect(buffer, send, recv):
        return to_partner(buffer, buffer, send, recv, other)

    columns_of(pos_row, pos_cols)
    columns_of(stamp_row, stamp_cols)
    write_requests(
        negatives, pos_row, pos_cols, owned, met_ids, asks, slot_cols, rank_cols
    )
    asked[pl.ds(0, 1), :] = asks[pl.ds(0, 1), :]
    loads[0].wait()
    pl.semaphore_wait(barrier, DEVICES - 1)

    each_partner(
        lambda group, item, device: to_partner(
            asks.at[pl.ds(group * GROUP + item, 1)],
            asked.at[pl.ds(group * GROUP + item, 1)],
            ask_send,
            ask_recv.at[group],
            device,
        ).start()
    )
    place = lax.rem(seq, 4)
    quarter = TOKENS // 4

    def shifted(steps):
        return (lax.rem(seq + 32 + steps, 32), loop)

    def halo(at, source, target, device):
        return to_partner(source, target, halo_send.at[at], halo_recv.at[at], device)

    def piece(source, part, device):
        rows = pl.ds(part * quarter, quarter)
        return halo(1, far.at[source, rows], far.at[1, rows], device)

    near_halos = [
        (place < 3, halo(0, events, far.at[0], shifted(1))),
        (place == 3, halo(3, events, far.at[3], shifted(4))),
        (place < 4, halo(2, events, far.at[2], shifted(3))),
    ]
    corner = [(place == 3, halo(0, far.at[3], far.at[0], shifted(-3)))]
    forward = [
        (place < 4, piece(0, 0, shifted(1))),
        (place < 3, piece(0, 1, shifted(1))),
        (place == 2, piece(0, 2, shifted(1))),
    ]
    backward = [
        (place == 1, piece(2, 1, shifted(-1))),
        (place > 0, piece(2, 2, shifted(-1))),
        (place < 4, piece(2, 3, shifted(-1))),
    ]

    def start_all(copies):
        for when, copy in copies:
            pl.when(when)(copy.start)

    def await_halo(at):
        halo(at, far.at[at], far.at[at], other).wait_recv()

    start_all(near_halos)

    lanes_of(met_ids, neg_ids, PER_OWNER, 0)
    loads[1].wait()
    widen_table(units, lines)
    def send_group(group, target, base, send, recv):
        for item, device in enumerate(partners(group)):

            def start(item=item, device=device):
                to_partner(
                    sent.at[group * GROUP + item],
                    target.at[(group - base) * GROUP + item],
                    send,
                    recv.at[group],
                    device,
                ).start()

            if item == 0:
                pl.when(group > 0)(start)
            else:
                start()

    def keep_own(target):
        mine = pltpu.make_async_copy(sent.at[0], target.at[0], local_sem)
        mine.start()
        mine.wait()

    def await_group(group, target, send, recv):
        @pl.when(group == 0)
        def _():
            expect(target.at[pl.ds(1, GROUP - 1)], send, recv.at[0]).wait_recv()

        @pl.when(group > 0)
        def _():
            expect(target.at[pl.ds(0, GROUP)], send, recv.at[group]).wait_recv()

    def answer_group(group, _):
        start = pl.multiple_of(group * GROUP, GROUP)
        await_group(group, asked, ask_send, ask_recv)
        scalars = pltpu.make_async_copy(
            asked.at[pl.ds(start, GROUP)], asked_scalar.at[pl.ds(start, GROUP)], local_sem
        )
        scalars.start()
        scalars.wait()

        def one(item, _):
            answer(asked_scalar, lines, stage, sent, group * GROUP + item)
            return 0

        lax.fori_loop(0, GROUP, one, 0)
        send_group(group, answered, 0, row_send, row_recv)
        @pl.when(group == CORNER_TURN)
        def _():
            pl.when(place == 3)(functools.partial(await_halo, 3))
            start_all(corner)

        @pl.when(group == BACK_TURN)
        def _():
            await_halo(2)
            start_all(backward)

        @pl.when(group == FORWARD_TURN)
        def _():
            await_halo(0)
            start_all(forward)

        return 0

    lax.fori_loop(0, GROUPS, answer_group, 0)
    keep_own(answered)
    loads[2].wait()
    project_own(events, in_gain, w_in, gate, queries, keys, values)
    sums[...] = jnp.zeros_like(sums)
    targets[...] = jnp.zeros_like(targets)
    d_state[...] = jnp.zeros_like(d_state)
    lanes_of(asked, neg_asked, PER_OWNER, 0)
    lanes_of(asked, pos_asked, CAPACITY, PER_OWNER)
    await_halo(1)

    def far_block(reach, _):
        live = jnp.where(seq >= reach, 1.0, 0.0).astype(F32)
        project_far(reach, far[reach - 1], live, in_gain, w_in, keys, values)
        return 0

    lax.fori_loop(1, WINDOW, far_block, 0)
    attend(stamp_cols, stamp_row, queries, keys, values, mixed)
    loads[3].wait()
    loads[4].wait()
    finish_hidden(events, carried, attn_gain, w_out, gate, mixed, hidden)
    unit_hidden(hidden, hidden_unit)

    def meet(group, _):
        await_group(group, answered, row_send, row_recv)
        meet_group(
            group, answered, neg_ids, pos_cols, slot_cols, hidden_unit, units, lines, sums, targets
        )
        return 0

    lax.fori_loop(0, GROUPS, meet, 0)
    d_pos[...] = settle(hidden_unit, sums, targets, loss, inverse)
    expect(sent.at[pl.ds(0, DEVICES - 1)], row_send, row_recv.at[0]).wait_send()

    def back(group, _):
        return_group(
            group, answered, slot_cols, hidden_unit, units, lines, inverse, d_pos, d_state, sent
        )
        send_group(group, returned, 0, back_send, back_recv)
        return 0

    lax.fori_loop(0, GROUPS - 1, back, 0)

    def back_last(group, _):
        return_group(
            group, answered, slot_cols, hidden_unit, units, lines, inverse, d_pos, d_state, sent
        )
        send_group(group, last, GROUPS - 1, back_send, back_recv)
        return 0

    lax.fori_loop(GROUPS - 1, GROUPS, back_last, 0)
    keep_own(returned)
    hidden_back(hidden, d_state, targets, grad)
    total[...] = jnp.zeros_like(total)

    def collect(pair, _):
        await_group(2 * pair, returned, back_send, back_recv)
        await_group(2 * pair + 1, returned, back_send, back_recv)
        add_groups([2 * pair, 2 * pair + 1], returned, neg_asked, pos_asked, total)
        return 0

    lax.fori_loop(0, GROUPS // 2 - 1, collect, 0)
    left = jnp.int32(GROUPS - 2)
    await_group(left, returned, back_send, back_recv)
    add_groups([left], returned, neg_asked, pos_asked, total)
    expect(asked.at[pl.ds(1, DEVICES - 1)], ask_send, ask_recv.at[0]).wait_send()
    for when, copy in near_halos + corner + forward + backward:
        pl.when(when)(copy.wait_send)
    expect(sent.at[pl.ds(0, DEVICES - 1)], back_send, back_recv.at[0]).wait_send()
    expect(last, back_send, back_recv.at[GROUPS - 1]).wait_recv()


def whole(kind, shape):
    return pltpu.VMEM(shape, kind)


def on_device(events, carried, positions, neg_ids, pos_ids, in_gain, w_in, attn_gain, w_out, table):
    inside = pl.BlockSpec(memory_space=pltpu.VMEM)
    outside = pl.BlockSpec(memory_space=pl.ANY)
    integers = jnp.int32
    loss, grad_hidden, most, last, neg_asked, pos_asked = pl.pallas_call(
        step_kernel,
        out_shape=(
            pltpu.VMEM((TOKENS // LANES, LANES), F32),
            pltpu.VMEM((TOKENS, WIDTH), BF16),
            pltpu.VMEM((ROWS, WIDTH), F32),
            pltpu.VMEM((GROUP, MESSAGE, LANES), BF16),
            pltpu.VMEM((GROUPS * BANDS, LANES), integers),
            pltpu.VMEM((GROUPS, LANES), integers),
        ),
        in_specs=[
            outside,
            outside,
            inside,
            inside,
            inside,
            inside,
            outside,
            inside,
            outside,
            outside,
        ],
        out_specs=(inside,) * 6,
        scratch_shapes=[
            whole(BF16, (TOKENS, WIDTH)),
            whole(F32, (TOKENS, WIDTH)),
            whole(BF16, (WIDTH, 4 * WIDTH)),
            whole(BF16, (WIDTH, WIDTH)),
            whole(BF16, (WINDOW, TOKENS, WIDTH)),
            whole(integers, (TOKENS, LANES)),
            whole(integers, (TOKENS, LANES)),
            whole(integers, (TOKENS, LANES)),
            whole(integers, (TOKENS, LANES)),
            whole(integers, (DEVICES, LANES)),
            whole(integers, (DEVICES, LANES)),
            whole(integers, (DEVICES, LANES)),
            whole(integers, (DEVICES, LANES)),
            pltpu.SMEM((DEVICES, LANES), integers),
            whole(integers, (GROUPS * BANDS, LANES)),
            whole(F32, (ROWS * BANDS, LANES)),
            whole(BF16, (ROWS, WIDTH)),
            whole(F32, (MESSAGE, LANES)),
            whole(BF16, (DEVICES, MESSAGE, LANES)),
            whole(BF16, (DEVICES, MESSAGE, LANES)),
            whole(BF16, (DEVICES - GROUP, MESSAGE, LANES)),
            whole(BF16, (TOKENS, WIDTH)),
            whole(BF16, (BANDS, TOKENS, LANES)),
            whole(BF16, (WINDOW, BANDS, TOKENS, LANES)),
            whole(BF16, (WINDOW, BANDS, TOKENS, LANES)),
            whole(F32, (BANDS, TOKENS, LANES)),
            whole(BF16, (TOKENS, WIDTH)),
            whole(BF16, (TOKENS, WIDTH)),
            whole(F32, (TOKENS, LANES)),
            whole(F32, (TOKENS, WIDTH)),
            whole(F32, (TOKENS, LANES)),
            whole(BF16, (TOKENS, WIDTH)),
            whole(F32, (TOKENS, WIDTH)),
            pltpu.SemaphoreType.DMA((5,)),
            pltpu.SemaphoreType.DMA,
            pltpu.SemaphoreType.DMA,
            pltpu.SemaphoreType.DMA((GROUPS,)),
            pltpu.SemaphoreType.DMA((4,)),
            pltpu.SemaphoreType.DMA((4,)),
            pltpu.SemaphoreType.DMA,
            pltpu.SemaphoreType.DMA((GROUPS,)),
            pltpu.SemaphoreType.DMA,
            pltpu.SemaphoreType.DMA((GROUPS,)),
        ],
        compiler_params=pltpu.CompilerParams(
            collective_id=0, has_side_effects=True, vmem_limit_bytes=52 * 2**20
        ),
        name="step",
    )(
        events[0],
        carried[0],
        positions,
        neg_ids.reshape(NEG // LANES, LANES),
        pos_ids,
        in_gain[None, :],
        w_in,
        attn_gain[None, :],
        w_out,
        table,
    )
    fixed = [most, last, neg_asked, pos_asked, loss, grad_hidden]
    tile = pl.BlockSpec((END_TILE, WIDTH), lambda index: (index, 0))
    rest = [pl.BlockSpec(array.shape, lambda index: (0, 0)) for array in (loss, grad_hidden)]
    grad_table, loss, grad_hidden = pl.pallas_call(
        finish_kernel,
        grid=(ROWS // END_TILE,),
        out_shape=(
            jax.ShapeDtypeStruct((ROWS, WIDTH), F32),
            jax.ShapeDtypeStruct(loss.shape, F32),
            jax.ShapeDtypeStruct(grad_hidden.shape, BF16),
        ),
        in_specs=[inside] * 6,
        out_specs=[tile] + rest,
        compiler_params=pltpu.CompilerParams(vmem_limit_bytes=24 * 2**20),
        name="finish",
    )(*fixed)
    return (loss.reshape(1, TOKENS), grad_hidden[None], grad_table)


def solution(mesh):
    return jax.shard_map(
        on_device,
        mesh=mesh,
        in_specs=(
            P("loop", "seq", None),
            P("loop", "seq", None),
            P("loop", "seq"),
            P("loop", "seq", None),
            P("loop", "seq"),
            P(),
            P(),
            P(),
            P(),
            P(("seq", "loop"), None),
        ),
        out_specs=(P("loop", "seq"), P("loop", "seq", None), P(("seq", "loop"), None)),
        check_vma=False,
    )
```

```python
import functools

import jax
import jax.numpy as jnp
from jax import lax
from jax.experimental import pallas as pl
from jax.experimental.pallas import tpu as pltpu
from jax.sharding import PartitionSpec as P

HEADS = 8
DH = 64
WINDOW = 4
WIDTH = HEADS * DH
LANES = 128
BANDS = WIDTH // LANES
TOKENS = 512
NEG = 4096
ROWS = 4096
DEVICES = 128
PER_OWNER = NEG // DEVICES
CAPACITY = 2 * TOKENS // DEVICES
ASKED = PER_OWNER + CAPACITY
MESSAGE = ASKED * BANDS
GROUP = 16
GROUPS = DEVICES // GROUP
GROUP_NEG = GROUP * PER_OWNER
GROUP_POS = GROUP * CAPACITY
NEG_LINES = PER_OWNER * BANDS

SHARPNESS = 50.0
LOG2E = 1.4426950408889634
EPSILON = 1e-06
F32 = jnp.float32
BF16 = jnp.bfloat16
NT = (((1,), (1,)), ((), ()))
TN = (((0,), (0,)), ((), ()))
TILE = 1024
END_TILE = 512
HELD = 8
SAME_X = (0, 1, 4, 5)
OTHER_X = (2, 3, 6, 7, 8, 9, 10, 11, 12, 13, 14, 15)
CORNER_TURN, BACK_TURN, FORWARD_TURN = 4, 0, 1
BANK = 62 * 2**20


def silu(value):
    half = value * 0.5
    return half + half * jnp.tanh(half)


def row_sum(value):
    return jnp.sum(value, axis=-1, keepdims=True)


def normalise(rows, gain):
    wide = rows.astype(F32)
    scale = lax.rsqrt(row_sum(wide * wide) * (1.0 / WIDTH) + EPSILON)
    return (wide * scale * gain).astype(BF16)


def store_bands(ref, lead, value):
    for band in range(BANDS):
        ref[lead + (band,)] = value[:, band * LANES : (band + 1) * LANES]


def project_own(events, gain, w_in, gate, queries, keys, values):
    normed = normalise(events[...], gain[...])

    def column(index):
        part = jnp.dot(
            normed, w_in[:, index * WIDTH : (index + 1) * WIDTH], preferred_element_type=F32
        )
        return silu(part).astype(BF16)

    gate[...] = column(0)
    store_bands(values, (0,), column(1))
    store_bands(queries, (), (column(2).astype(F32) * 0.0625).astype(BF16))
    store_bands(keys, (0,), column(3))


def project_far(reach, rows, live, gain, w_in, keys, values):
    normed = normalise(rows, gain[...])

    def column(index):
        part = jnp.dot(
            normed, w_in[:, index * WIDTH : (index + 1) * WIDTH], preferred_element_type=F32
        )
        return (silu(part) * live).astype(BF16)

    store_bands(values, (reach,), column(1))
    store_bands(keys, (reach,), column(3))


def attend(stamp_cols, stamp_row, queries, keys, values, mixed):
    allowed = stamp_row[...] <= stamp_cols[:, :1]
    first = lax.broadcasted_iota(jnp.int32, (TOKENS, LANES), 1) < DH

    def pair(band, _):
        both = queries[band].astype(F32)
        parts = [
            jnp.where(first, both, 0.0).astype(BF16),
            jnp.where(first, 0.0, both).astype(BF16),
        ]

        def block(index, own):
            outs = []
            for part in parts:
                half = lax.dot_general(part, keys[index, band], NT, preferred_element_type=F32)
                weight = half + half * jnp.tanh(half)
                if own:
                    weight = jnp.where(allowed, weight, 0.0)
                outs.append(
                    jnp.dot(weight.astype(BF16), values[index, band], preferred_element_type=F32)
                )
            return jnp.where(first, outs[0], outs[1])

        mixed[band] = block(0, True)

        def later(index, _):
            mixed[band] += block(index, False)
            return 0

        lax.fori_loop(1, WINDOW, later, 0)
        return 0

    lax.fori_loop(0, BANDS, pair, 0)


def finish_hidden(events, carried, gain, w_out, gate, mixed, hidden):
    parts = [
        carried[:, band * LANES : (band + 1) * LANES] + mixed[band] for band in range(BANDS)
    ]
    squares = sum(row_sum(part * part) for part in parts)
    scale = lax.rsqrt(squares * (1.0 / WIDTH) + EPSILON)
    attended = jnp.concatenate(parts, axis=1)
    gated = (attended * scale * gain[...] * gate[...].astype(F32)).astype(BF16)
    hidden[...] = (
        events[...].astype(F32) + jnp.dot(gated, w_out[...], preferred_element_type=F32)
    ).astype(BF16)


def widen_table(table, lines):
    step = 256

    def part(index, _):
        start = pl.multiple_of(index * step, step)
        rows = table[pl.ds(start, step), :].astype(F32)
        for band in range(BANDS):
            lines[pl.ds(start * BANDS + band, step, stride=BANDS), :] = rows[
                :, band * LANES : (band + 1) * LANES
            ]
        return 0

    lax.fori_loop(0, ROWS // step, part, 0)


def answer(asked, lines, stage, message, peer):
    for slot in range(ASKED):
        row = jnp.maximum(asked[peer, slot], 0)
        stage[pl.ds(slot * BANDS, BANDS), :] = lines[pl.ds(row * BANDS, BANDS), :]
    for band in range(BANDS):
        message[peer, pl.ds(band * PER_OWNER, PER_OWNER), :] = stage[
            pl.ds(band, PER_OWNER, stride=BANDS), :
        ].astype(BF16)
    tail = [
        stage[pl.ds(NEG_LINES + band, CAPACITY, stride=BANDS), :] for band in range(BANDS)
    ]
    message[peer, pl.ds(NEG_LINES, CAPACITY * BANDS), :] = jnp.concatenate(tail, axis=0).astype(
        BF16
    )


def neg_rows(message, group):
    start = pl.multiple_of(group * GROUP, GROUP)
    parts = [
        message[pl.ds(start, GROUP), pl.ds(band * PER_OWNER, PER_OWNER), :].reshape(
            GROUP_NEG, LANES
        )
        for band in range(BANDS)
    ]
    return jnp.concatenate(parts, axis=1)


def pos_rows(message, group):
    start = pl.multiple_of(group * GROUP, GROUP)
    block = message[pl.ds(start, GROUP), pl.ds(NEG_LINES, CAPACITY * BANDS), :].astype(F32)
    block = block.reshape(GROUP, BANDS, CAPACITY, LANES)
    parts = [block[:, band].reshape(GROUP_POS, LANES) for band in range(BANDS)]
    return jnp.concatenate(parts, axis=1)


def unit_hidden(hidden, hidden_unit):
    wide = hidden[...].astype(F32)
    scale = lax.rsqrt(row_sum(wide * wide) + EPSILON)
    hidden_unit[...] = (wide * scale).astype(BF16)


def pick(slot_cols, group):
    lane = lax.broadcasted_iota(jnp.int32, (TOKENS, GROUP_POS), 1) + group * GROUP_POS
    return jnp.where(slot_cols[...] == lane, 1.0, 0.0).astype(BF16)


def share_rows(group, band):
    return pl.ds(pl.multiple_of((group * BANDS + band) * TOKENS, TOKENS), TOKENS)


def unit_rows(group):
    return pl.ds(pl.multiple_of(group * GROUP_NEG, GROUP_NEG), GROUP_NEG)


def meet_group(group, message, neg_ids, pos_cols, slot_cols, hidden_unit, units, shares, sums, targets):
    wide = neg_rows(message, group).astype(F32)
    scale = lax.rsqrt(row_sum(wide * wide) + EPSILON)
    unit = (wide * scale).astype(BF16)
    units[unit_rows(group), :] = unit
    logits = lax.dot_general(hidden_unit[...], unit, NT, preferred_element_type=F32)
    total = sums[...]
    for band in range(BANDS):
        keep = neg_ids[pl.ds(group * BANDS + band, 1), :] != pos_cols[...]
        near = logits[:, band * LANES : (band + 1) * LANES]
        grown = jnp.where(keep, jnp.exp2(near * (SHARPNESS * LOG2E)), 0.0)
        shares[share_rows(group, band), :] = grown
        total = total + grown
    sums[...] = total
    targets[...] += jnp.dot(
        pick(slot_cols, group),
        pos_rows(message, group).astype(BF16),
        preferred_element_type=F32,
    )


def settle(hidden_unit, sums, targets, loss, inverse):
    state = hidden_unit[...].astype(F32)
    wide = targets[...]
    scale = lax.rsqrt(row_sum(wide * wide) + EPSILON)
    unit = wide * scale
    logit = row_sum(state * unit) * SHARPNESS
    grown = jnp.exp(logit)
    total = grown + row_sum(sums[...])
    lost = jnp.broadcast_to(jnp.log(total) - logit, (TOKENS, LANES))
    for part in range(TOKENS // LANES):
        loss[pl.ds(part, 1), :] = lost[part * LANES : (part + 1) * LANES].T[:1]
    share = grown / total - 1.0
    inverse[...] = jnp.broadcast_to(1.0 / total, (TOKENS, LANES))
    upstream = (share * SHARPNESS) * state
    back = scale * (upstream - unit * row_sum(unit * upstream))
    targets[...] = (share * SHARPNESS) * unit
    return back.astype(BF16)


def return_group(group, message, slot_cols, hidden_unit, units, shares, inverse, d_pos, d_state, out):
    share = jnp.concatenate(
        [
            (shares[share_rows(group, band), :] * inverse[...]).astype(BF16)
            for band in range(BANDS)
        ],
        axis=1,
    )
    wide = neg_rows(message, group).astype(F32)
    scale = lax.rsqrt(row_sum(wide * wide) + EPSILON)
    unit = wide * scale
    upstream = (
        lax.dot_general(share, hidden_unit[...], TN, preferred_element_type=F32) * SHARPNESS
    )
    back = (scale * (upstream - unit * row_sum(unit * upstream))).astype(BF16)
    start = pl.multiple_of(group * GROUP, GROUP)
    for band in range(BANDS):
        out[pl.ds(start, GROUP), pl.ds(band * PER_OWNER, PER_OWNER), :] = back[
            :, band * LANES : (band + 1) * LANES
        ].reshape(GROUP, PER_OWNER, LANES)
    returned = lax.dot_general(pick(slot_cols, group), d_pos[...], TN, preferred_element_type=F32)
    parts = [
        returned[:, band * LANES : (band + 1) * LANES].reshape(GROUP, 1, CAPACITY, LANES)
        for band in range(BANDS)
    ]
    out[pl.ds(start, GROUP), pl.ds(NEG_LINES, CAPACITY * BANDS), :] = (
        jnp.concatenate(parts, axis=1).reshape(GROUP, CAPACITY * BANDS, LANES).astype(BF16)
    )
    d_state[...] += jnp.dot(share, units[unit_rows(group), :], preferred_element_type=F32)


def hidden_back(hidden, d_state, targets, grad):
    wide = hidden[...].astype(F32)
    scale = lax.rsqrt(row_sum(wide * wide) + EPSILON)
    unit = wide * scale
    upstream = d_state[...] * SHARPNESS + targets[...]
    grad[...] = (scale * (upstream - unit * row_sum(unit * upstream))).astype(BF16)


def group_rows(message, groups):
    parts = [neg_rows(message, group) for group in groups]
    parts += [pos_rows(message, group).astype(BF16) for group in groups]
    return jnp.concatenate(parts, axis=0)


def add_tile(start, count, neg_asked, pos_asked, groups, rows):
    row = lax.broadcasted_iota(jnp.int32, (count, LANES), 0) + start

    def hits(asked, line):
        return jnp.where(row == asked[pl.ds(line, 1), :], 1.0, 0.0).astype(BF16)

    wide = [
        hits(neg_asked, group * BANDS + band) for group in groups for band in range(BANDS)
    ]
    wide += [hits(pos_asked, group) for group in groups]
    return jnp.dot(jnp.concatenate(wide, axis=1), rows, preferred_element_type=F32)


def add_groups(groups, message, neg_asked, pos_asked, total):
    rows = group_rows(message, groups)

    def tile(index, _):
        start = pl.multiple_of(index * TILE, TILE)
        total[pl.ds(start, TILE), :] += add_tile(start, TILE, neg_asked, pos_asked, groups, rows)
        return 0

    lax.fori_loop(0, ROWS // TILE, tile, 0)


def finish_kernel(before, message, neg_asked, pos_asked, loss_in, grad_in, total, loss, grad):
    index = pl.program_id(0)

    @pl.when(index == 0)
    def _():
        loss[...] = loss_in[...]
        grad[...] = grad_in[...]

    start = pl.multiple_of(index * END_TILE, END_TILE)
    total[...] = before[pl.ds(start, END_TILE), :] + add_tile(
        start,
        END_TILE,
        neg_asked,
        pos_asked,
        [GROUPS - 2, GROUPS - 1],
        group_rows(message, [0, 1]),
    )


SEQ_BITS = ("x0", "x1", "zl", "y0", "y1")
LOOP_BITS = ("c", "zh")
ITEM_FLIPS = (("y0", "zh", "c"), ("x0", "y1"), ("zl", "c"), ("x1", "zh"))
GROUP_FLIPS = ("c", "zh", "y1")


def own_bits():
    seq, loop = lax.axis_index("seq"), lax.axis_index("loop")
    bits = {name: lax.rem(lax.div(seq, 2**at), 2) for at, name in enumerate(SEQ_BITS)}
    bits.update({name: lax.rem(lax.div(loop, 2**at), 2) for at, name in enumerate(LOOP_BITS)})
    return bits


def partners(group):
    bits = own_bits()
    for at, name in enumerate(GROUP_FLIPS):
        turn = lax.rem(lax.div(group, 2**at), 2)
        bits[name] = bits[name] + turn - 2 * bits[name] * turn
    seq = sum(bits[name] * 2**at for at, name in enumerate(SEQ_BITS))
    loop = sum(bits[name] * 2**at for at, name in enumerate(LOOP_BITS))
    seq_turn = {name: (1 - 2 * bits[name]) * 2**at for at, name in enumerate(SEQ_BITS)}
    loop_turn = {name: (1 - 2 * bits[name]) * 2**at for at, name in enumerate(LOOP_BITS)}
    met = []
    for item in range(GROUP):
        flips = set()
        for at, names in enumerate(ITEM_FLIPS):
            if item >> at & 1:
                flips ^= set(names)
        met.append(
            (
                sum((seq_turn[name] for name in SEQ_BITS if name in flips), seq),
                sum((loop_turn[name] for name in LOOP_BITS if name in flips), loop),
            )
        )
    return met


def each_partner(act):
    def one(group, _):
        for item, device in enumerate(partners(group)):
            if item == 0:

                @pl.when(group > 0)
                def _():
                    act(group, item, device)

            else:
                act(group, item, device)
        return 0

    lax.fori_loop(0, GROUPS, one, 0)


def slot_of(owner):
    me = lax.axis_index("seq") * 4 + lax.axis_index("loop")
    apart = jnp.bitwise_xor(owner, me)
    names = LOOP_BITS + SEQ_BITS
    bit = {name: jnp.bitwise_and(jnp.right_shift(apart, at), 1) for at, name in enumerate(names)}
    first = jnp.bitwise_xor(jnp.bitwise_xor(bit["c"], bit["y0"]), bit["zl"])
    second = jnp.bitwise_xor(jnp.bitwise_xor(bit["zh"], bit["y0"]), bit["x1"])
    third = jnp.bitwise_xor(bit["y1"], bit["x0"])
    item = bit["y0"] + 2 * bit["x0"] + 4 * bit["zl"] + 8 * bit["x1"]
    return item + 16 * first + 32 * second + 64 * third


def columns_of(row, out):
    for part in range(TOKENS // LANES):
        square = jnp.broadcast_to(row[:, part * LANES : (part + 1) * LANES], (LANES, LANES))
        out[pl.ds(part * LANES, LANES), :] = square.T


def lanes_of(rows, out, count, skip):
    lane = lax.broadcasted_iota(jnp.int32, (GROUPS, LANES), 1)
    bands = count * GROUP // LANES
    share = LANES // count
    for band in range(bands):
        packed = jnp.zeros((GROUPS, LANES), jnp.int32)
        for part in range(share):
            some = rows[pl.ds(band * share + part, GROUPS, stride=GROUP), :]
            some = pltpu.roll(some, (part * count - skip) % LANES, axis=1)
            inside = (lane >= part * count) & (lane < (part + 1) * count)
            packed = jnp.where(inside, some, packed)
        out[pl.ds(band, GROUPS, stride=bands), :] = packed


def count_rows(flags):
    rows = flags.shape[0]
    while rows > 8:
        rows //= 2
        flags = flags[:rows] + flags[rows:]
    total = flags[:1]
    for row in range(1, 8):
        total = total + flags[row : row + 1]
    return total


def write_requests(negatives, pos_row, pos_cols, owned, met_ids, asks, slot_cols, rank_cols):
    lane = lax.broadcasted_iota(jnp.int32, (TOKENS, LANES), 1)
    line = lax.broadcasted_iota(jnp.int32, (TOKENS, LANES), 0)
    ids = pos_cols[...]
    slot = slot_of(jnp.right_shift(ids, 12))
    slot_row = slot_of(jnp.right_shift(pos_row[...], 12))
    ranks = []
    for part in range(TOKENS // LANES):
        near = slot_row[:, part * LANES : (part + 1) * LANES]
        earlier = (slot == near) & (line < lane + part * LANES)
        ranks.append(count_rows(jnp.where(earlier, 1, 0)))
    columns_of(jnp.concatenate(ranks, axis=1), rank_cols)
    rank = rank_cols[...]
    slot_cols[...] = slot * CAPACITY + rank
    named = jnp.where(slot == lane, jnp.bitwise_and(ids, ROWS - 1) + 1, 0)
    wanted = [jnp.zeros((PER_OWNER, LANES), jnp.int32)]
    for place in range(CAPACITY):
        wanted.append(count_rows(jnp.where(rank == place, named, 0)))
    wanted.append(jnp.zeros((LANES - ASKED, LANES), jnp.int32))
    wanted = jnp.concatenate(wanted, axis=0).T - 1
    share = LANES // PER_OWNER
    for part in range(share):
        owned[pl.ds(part, DEVICES // share, stride=share), :] = pltpu.roll(
            negatives[...], (LANES - part * PER_OWNER) % LANES, axis=1
        )

    def order(group, _):
        for item, (seq, loop) in enumerate(partners(group)):
            met_ids[pl.ds(group * GROUP + item, 1), :] = owned[pl.ds(seq * 4 + loop, 1), :]
        return 0

    lax.fori_loop(0, GROUPS, order, 0)
    slots = lax.broadcasted_iota(jnp.int32, (DEVICES, LANES), 1)
    asks[...] = jnp.where(
        slots < PER_OWNER, jnp.bitwise_and(met_ids[...], ROWS - 1), wanted
    )


def step_kernel(
    events_in,
    carried_in,
    stamp_row,
    negatives,
    pos_row,
    in_gain,
    w_in_in,
    attn_gain,
    w_out_in,
    table,
    loss,
    grad,
    total,
    last,
    neg_asked,
    pos_asked,
    events,
    carried,
    w_in,
    w_out,
    far,
    stamp_cols,
    pos_cols,
    slot_cols,
    rank_cols,
    owned,
    met_ids,
    asks,
    asked,
    asked_scalar,
    neg_ids,
    lines,
    units,
    stage,
    sent,
    answered,
    returned,
    gate,
    queries,
    keys,
    values,
    mixed,
    hidden,
    hidden_unit,
    sums,
    targets,
    inverse,
    d_pos,
    d_state,
    load_sems,
    local_sem,
    ask_send,
    ask_recv,
    halo_send,
    halo_recv,
    row_send,
    row_recv,
    back_send,
    back_recv,
):
    seq, loop = lax.axis_index("seq"), lax.axis_index("loop")
    barrier = pltpu.get_barrier_semaphore()
    each_partner(
        lambda group, item, device: pl.semaphore_signal(
            barrier, inc=1, device_id=device, device_id_type=pl.DeviceIdType.MESH
        )
    )
    loads = [
        pltpu.make_async_copy(source, target, load_sems.at[at])
        for at, (source, target) in enumerate(
            [
                (events_in, events),
                (table, units),
                (w_in_in, w_in),
                (w_out_in, w_out),
                (carried_in, carried),
            ]
        )
    ]
    for load in loads:
        load.start()

    def to_partner(source, target, send, recv, device):
        return pltpu.make_async_remote_copy(
            src_ref=source,
            dst_ref=target,
            send_sem=send,
            recv_sem=recv,
            device_id=device,
            device_id_type=pl.DeviceIdType.MESH,
        )

    other = (seq, loop + 1 - 2 * lax.rem(loop, 2))

    def expect(buffer, send, recv):
        return to_partner(buffer, buffer, send, recv, other)

    columns_of(pos_row, pos_cols)
    columns_of(stamp_row, stamp_cols)
    write_requests(
        negatives, pos_row, pos_cols, owned, met_ids, asks, slot_cols, rank_cols
    )
    asked[pl.ds(0, 1), :] = asks[pl.ds(0, 1), :]
    loads[0].wait()
    pl.semaphore_wait(barrier, DEVICES - 1)

    each_partner(
        lambda group, item, device: to_partner(
            asks.at[pl.ds(group * GROUP + item, 1)],
            asked.at[pl.ds(group * GROUP + item, 1)],
            ask_send,
            ask_recv.at[group],
            device,
        ).start()
    )
    place = lax.rem(seq, 4)
    quarter = TOKENS // 4

    def shifted(steps):
        return (lax.rem(seq + 32 + steps, 32), loop)

    def halo(at, source, target, device):
        return to_partner(source, target, halo_send.at[at], halo_recv.at[at], device)

    def piece(source, part, device):
        rows = pl.ds(part * quarter, quarter)
        return halo(1, far.at[source, rows], far.at[1, rows], device)

    near_halos = [
        (place < 3, halo(0, events, far.at[0], shifted(1))),
        (place == 3, halo(3, events, far.at[3], shifted(4))),
        (place < 4, halo(2, events, far.at[2], shifted(3))),
    ]
    corner = [(place == 3, halo(0, far.at[3], far.at[0], shifted(-3)))]
    forward = [
        (place > 0, piece(0, 0, shifted(1))),
        ((place == 1) | (place == 2), piece(0, 1, shifted(1))),
        (place == 2, piece(0, 2, shifted(1))),
    ]
    backward = [
        (place == 2, piece(2, 0, shifted(-1))),
        ((place == 1) | (place == 2), piece(2, 1, shifted(-1))),
        (place > 0, piece(2, 2, shifted(-1))),
        (place < 4, piece(2, 3, shifted(-1))),
    ]

    def start_all(copies):
        for when, copy in copies:
            pl.when(when)(copy.start)

    def await_halo(at):
        halo(at, far.at[at], far.at[at], other).wait_recv()

    start_all(near_halos)

    lanes_of(met_ids, neg_ids, PER_OWNER, 0)
    loads[1].wait()
    widen_table(units, lines)
    def send_group(group, target, base, send, recv, items=range(GROUP)):
        for item, device in enumerate(partners(group)):
            if item not in items:
                continue

            def start(item=item, device=device):
                to_partner(
                    sent.at[group * GROUP + item],
                    target.at[(group - base) * GROUP + item],
                    send,
                    recv.at[group],
                    device,
                ).start()

            if item == 0:
                pl.when(group > 0)(start)
            else:
                start()

    def keep_own(target):
        mine = pltpu.make_async_copy(sent.at[0], target.at[0], local_sem)
        mine.start()
        mine.wait()

    def await_group(group, target, send, recv):
        @pl.when(group == 0)
        def _():
            expect(target.at[pl.ds(1, GROUP - 1)], send, recv.at[0]).wait_recv()

        @pl.when(group > 0)
        def _():
            expect(target.at[pl.ds(0, GROUP)], send, recv.at[group]).wait_recv()

    def answer_group(group, _):
        start = pl.multiple_of(group * GROUP, GROUP)
        await_group(group, asked, ask_send, ask_recv)
        scalars = pltpu.make_async_copy(
            asked.at[pl.ds(start, GROUP)], asked_scalar.at[pl.ds(start, GROUP)], local_sem
        )
        scalars.start()
        scalars.wait()

        def one(item, _):
            answer(asked_scalar, lines, stage, sent, group * GROUP + item)
            return 0

        lax.fori_loop(0, GROUP, one, 0)
        @pl.when(group == CORNER_TURN)
        def _():
            pl.when(place == 3)(functools.partial(await_halo, 3))
            start_all(corner)

        early = group < HELD

        @pl.when(early)
        def _():
            send_group(group, answered, 0, row_send, row_recv, SAME_X)

        @pl.when(group >= HELD)
        def _():
            send_group(group, answered, 0, row_send, row_recv)

        return 0

    def send_held(group, _):
        @pl.when(group == BACK_TURN)
        def _():
            await_halo(2)
            start_all(backward)

        @pl.when(group == FORWARD_TURN)
        def _():
            pl.when(place > 0)(functools.partial(await_halo, 0))
            start_all(forward)

        send_group(group, answered, 0, row_send, row_recv, OTHER_X)
        return 0

    lax.fori_loop(0, HELD, answer_group, 0)
    lax.fori_loop(0, HELD, send_held, 0)
    lax.fori_loop(HELD, GROUPS, answer_group, 0)
    keep_own(answered)
    loads[2].wait()
    project_own(events, in_gain, w_in, gate, queries, keys, values)
    sums[...] = jnp.zeros_like(sums)
    targets[...] = jnp.zeros_like(targets)
    d_state[...] = jnp.zeros_like(d_state)
    total[...] = jnp.zeros_like(total)
    lanes_of(asked, neg_asked, PER_OWNER, 0)
    lanes_of(asked, pos_asked, CAPACITY, PER_OWNER)
    await_halo(1)
    pl.when(place == 0)(functools.partial(await_halo, 0))

    def far_block(reach, _):
        live = jnp.where(seq >= reach, 1.0, 0.0).astype(F32)
        project_far(reach, far[reach - 1], live, in_gain, w_in, keys, values)
        return 0

    lax.fori_loop(1, WINDOW, far_block, 0)
    attend(stamp_cols, stamp_row, queries, keys, values, mixed)
    loads[3].wait()
    loads[4].wait()
    finish_hidden(events, carried, attn_gain, w_out, gate, mixed, hidden)
    unit_hidden(hidden, hidden_unit)

    def meet(group, _):
        await_group(group, answered, row_send, row_recv)
        meet_group(
            group, answered, neg_ids, pos_cols, slot_cols, hidden_unit, units, lines, sums, targets
        )
        return 0

    lax.fori_loop(0, GROUPS, meet, 0)
    d_pos[...] = settle(hidden_unit, sums, targets, loss, inverse)
    expect(sent.at[pl.ds(0, DEVICES - 1)], row_send, row_recv.at[0]).wait_send()

    def back(group, _):
        return_group(
            group, answered, slot_cols, hidden_unit, units, lines, inverse, d_pos, d_state, sent
        )
        send_group(group, returned, 0, back_send, back_recv)
        return 0

    lax.fori_loop(0, GROUPS - 2, back, 0)

    def back_last(group, _):
        return_group(
            group, answered, slot_cols, hidden_unit, units, lines, inverse, d_pos, d_state, sent
        )
        send_group(group, last, GROUPS - 2, back_send, back_recv)
        return 0

    lax.fori_loop(GROUPS - 2, GROUPS, back_last, 0)
    keep_own(returned)
    hidden_back(hidden, d_state, targets, grad)

    def collect(pair, _):
        await_group(2 * pair, returned, back_send, back_recv)
        await_group(2 * pair + 1, returned, back_send, back_recv)
        add_groups([2 * pair, 2 * pair + 1], returned, neg_asked, pos_asked, total)
        return 0

    lax.fori_loop(0, GROUPS // 2 - 1, collect, 0)
    expect(asked.at[pl.ds(1, DEVICES - 1)], ask_send, ask_recv.at[0]).wait_send()
    for when, copy in near_halos + corner + forward + backward:
        pl.when(when)(copy.wait_send)
    expect(sent.at[pl.ds(0, DEVICES - 1)], back_send, back_recv.at[0]).wait_send()
    for end in range(2):
        expect(
            last.at[pl.ds(end * GROUP, GROUP)], back_send, back_recv.at[GROUPS - 2 + end]
        ).wait_recv()


def whole(kind, shape):
    return pltpu.VMEM(shape, kind)


def on_device(events, carried, positions, neg_ids, pos_ids, in_gain, w_in, attn_gain, w_out, table):
    inside = pl.BlockSpec(memory_space=pltpu.VMEM)
    outside = pl.BlockSpec(memory_space=pl.ANY)
    integers = jnp.int32
    loss, grad_hidden, most, last, neg_asked, pos_asked = pl.pallas_call(
        step_kernel,
        out_shape=(
            pltpu.VMEM((TOKENS // LANES, LANES), F32),
            pltpu.VMEM((TOKENS, WIDTH), BF16),
            pltpu.VMEM((ROWS, WIDTH), F32),
            pltpu.VMEM((2 * GROUP, MESSAGE, LANES), BF16),
            pltpu.VMEM((GROUPS * BANDS, LANES), integers),
            pltpu.VMEM((GROUPS, LANES), integers),
        ),
        in_specs=[
            outside,
            outside,
            inside,
            inside,
            inside,
            inside,
            outside,
            inside,
            outside,
            outside,
        ],
        out_specs=(inside,) * 6,
        scratch_shapes=[
            whole(BF16, (TOKENS, WIDTH)),
            whole(F32, (TOKENS, WIDTH)),
            whole(BF16, (WIDTH, 4 * WIDTH)),
            whole(BF16, (WIDTH, WIDTH)),
            whole(BF16, (WINDOW, TOKENS, WIDTH)),
            whole(integers, (TOKENS, LANES)),
            whole(integers, (TOKENS, LANES)),
            whole(integers, (TOKENS, LANES)),
            whole(integers, (TOKENS, LANES)),
            whole(integers, (DEVICES, LANES)),
            whole(integers, (DEVICES, LANES)),
            whole(integers, (DEVICES, LANES)),
            whole(integers, (DEVICES, LANES)),
            pltpu.SMEM((DEVICES, LANES), integers),
            whole(integers, (GROUPS * BANDS, LANES)),
            whole(F32, (ROWS * BANDS, LANES)),
            whole(BF16, (ROWS, WIDTH)),
            whole(F32, (MESSAGE, LANES)),
            whole(BF16, (DEVICES, MESSAGE, LANES)),
            whole(BF16, (DEVICES, MESSAGE, LANES)),
            whole(BF16, (DEVICES - 2 * GROUP, MESSAGE, LANES)),
            whole(BF16, (TOKENS, WIDTH)),
            whole(BF16, (BANDS, TOKENS, LANES)),
            whole(BF16, (WINDOW, BANDS, TOKENS, LANES)),
            whole(BF16, (WINDOW, BANDS, TOKENS, LANES)),
            whole(F32, (BANDS, TOKENS, LANES)),
            whole(BF16, (TOKENS, WIDTH)),
            whole(BF16, (TOKENS, WIDTH)),
            whole(F32, (TOKENS, LANES)),
            whole(F32, (TOKENS, WIDTH)),
            whole(F32, (TOKENS, LANES)),
            whole(BF16, (TOKENS, WIDTH)),
            whole(F32, (TOKENS, WIDTH)),
            pltpu.SemaphoreType.DMA((5,)),
            pltpu.SemaphoreType.DMA,
            pltpu.SemaphoreType.DMA,
            pltpu.SemaphoreType.DMA((GROUPS,)),
            pltpu.SemaphoreType.DMA((4,)),
            pltpu.SemaphoreType.DMA((4,)),
            pltpu.SemaphoreType.DMA,
            pltpu.SemaphoreType.DMA((GROUPS,)),
            pltpu.SemaphoreType.DMA,
            pltpu.SemaphoreType.DMA((GROUPS,)),
        ],
        compiler_params=pltpu.CompilerParams(
            collective_id=0, has_side_effects=True, vmem_limit_bytes=52 * 2**20
        ),
        name="step",
    )(
        events[0],
        carried[0],
        positions,
        neg_ids.reshape(NEG // LANES, LANES),
        pos_ids,
        in_gain[None, :],
        w_in,
        attn_gain[None, :],
        w_out,
        table,
    )
    fixed = [most, last, neg_asked, pos_asked, loss, grad_hidden]
    tile = pl.BlockSpec((END_TILE, WIDTH), lambda index: (index, 0))
    rest = [pl.BlockSpec(array.shape, lambda index: (0, 0)) for array in (loss, grad_hidden)]
    grad_table, loss, grad_hidden = pl.pallas_call(
        finish_kernel,
        grid=(ROWS // END_TILE,),
        out_shape=(
            jax.ShapeDtypeStruct((ROWS, WIDTH), F32),
            jax.ShapeDtypeStruct(loss.shape, F32),
            jax.ShapeDtypeStruct(grad_hidden.shape, BF16),
        ),
        in_specs=[inside] * 6,
        out_specs=[tile] + rest,
        compiler_params=pltpu.CompilerParams(vmem_limit_bytes=24 * 2**20),
        name="finish",
    )(*fixed)
    return (loss.reshape(1, TOKENS), grad_hidden[None], grad_table)


def solution(mesh):
    return jax.shard_map(
        on_device,
        mesh=mesh,
        in_specs=(
            P("loop", "seq", None),
            P("loop", "seq", None),
            P("loop", "seq"),
            P("loop", "seq", None),
            P("loop", "seq"),
            P(),
            P(),
            P(),
            P(),
            P(("seq", "loop"), None),
        ),
        out_specs=(P("loop", "seq"), P("loop", "seq", None), P(("seq", "loop"), None)),
        check_vma=False,
    )
```
